256 devices in a mesh: row: 16 (over x, z_lo, core), col: 16 (over y, z_hi).
Axes of the slice: x: 4, y: 4, z: 8 (z_hi: 4, z_lo: 2; z = z_hi * 2 + z_lo), core: 2. Of those that a mesh axis runs over, the one named last changes fastest.
Arguments:
- features: bfloat16 [65536, 256], P(('row', 'col')), may hold values from -6 to 6
- weight: bfloat16 [256, 256], replicated, may hold values from -0.375 to 0.375
- adjacency: bfloat16 [16, 16, 192, 128, 128], P('row', 'col'), may hold values from 0 to 0.0625
- tile_row: int32 [16, 16, 192], P('row', 'col'), may hold values from 0 to 31
- tile_col: int32 [16, 16, 192], P('row', 'col'), may hold values from 0 to 31
- tile_count: int32 [16, 16], P('row', 'col'), may hold values from 24 to 192, as said below
- cotangent: bfloat16 [65536, 256], P(('row', 'col')), may hold values from -6 to 6
Outputs:
- output: bfloat16 [65536, 256], P(('row', 'col'))
- grad_weight: float32 [256, 256], replicated
- grad_input: bfloat16 [65536, 256], P(('row', 'col'))
The draws below stay inside these ranges and needn't reach their ends.
Inputs may be any that keep to these rules, and one draw needn't show every extreme that they name: `tile_count`: the busiest cell uses all 192 slots; the others use between 24 and 96.
All inputs are finite; a program needn't handle non-finite values.
Results may differ from the reference program's by a relative error of at most 0.0067.
Values may be sent and summed in bfloat16 or wider, within the bound.
A program may use at most 128 MiB of HBM per device.

```python
import jax
import jax.numpy as jnp
from jax import lax

F = 256
TILE = 128
S = 256
KMAX = 192
NODES = 65536
N_ROW = 16
N_COL = 16


def draw_tile_count(key, part):
    key = jax.random.fold_in(key, 7)
    first_key, second_key = jax.random.split(key)
    cells = N_ROW * N_COL
    base = jax.random.randint(first_key, (cells,), KMAX // 8, KMAX // 2 + 1)
    busiest = jax.random.randint(second_key, (), 0, cells)
    filled = jnp.where(jnp.arange(cells) == busiest, KMAX, base)
    return filled.reshape(N_ROW, N_COL).astype(jnp.int32)


def touch_ends(array, own_key, smallest, largest):
    longest = array.shape.index(max(array.shape))
    spots = []
    for shift in (0, 1):
        where = [jax.random.randint(jax.random.fold_in(own_key, axis), (), 0, length) for axis, length in enumerate(array.shape)]
        where[longest] = (where[longest] + shift) % array.shape[longest]
        spots.append(tuple(where))
    return array.at[spots[0]].set(smallest).at[spots[1]].set(largest)


def block_levels(rng, extent, cuts, least, high):
    factor_of = 1.0
    for dim, parts in cuts:
        heights = jax.random.uniform(jax.random.fold_in(jax.random.fold_in(rng, 6), dim), (parts,), jnp.float32, least / len(cuts), high / len(cuts))
        factor_of = factor_of * jnp.repeat(jnp.exp(heights), extent[dim] // parts).reshape((-1,) + (1,) * (len(extent) - 1 - dim))
    return factor_of


def scatter_about(own_key, shape, scale, reach, cuts=(), held_as=jnp.bfloat16):
    factor_of = block_levels(own_key, shape, cuts, -0.22, 0.18) if cuts else 1.0
    array = jax.random.normal(own_key, shape, jnp.float32) * scale * factor_of
    return jnp.minimum(jnp.maximum(array, -reach), reach).astype(held_as)


def setup_inputs(seed: int = 0) -> dict:
    streams_of = jax.random.split(jax.random.key(seed), 8)
    return {
        "features": scatter_about(streams_of[0], (NODES, F), 1.0, 6.0, ((0, 256),)),
        "weight": scatter_about(streams_of[1], (F, F), F ** -0.5, 0.375),
        "adjacency": jnp.clip(0.0625 * jax.random.uniform(streams_of[2], (N_ROW, N_COL, KMAX, TILE, TILE), jnp.float32) ** block_levels(streams_of[2], (N_ROW, N_COL, KMAX, TILE, TILE), ((0, 16), (1, 16)), -0.2, 0.2), 0.0, 0.0625).astype(jnp.bfloat16),
        "tile_row": touch_ends(jax.random.randint(streams_of[3], (N_ROW, N_COL, KMAX), 0, N_COL * S // TILE), jax.random.fold_in(streams_of[3], 1), 0, (N_COL * S // TILE) - 1).astype(jnp.int32),
        "tile_col": touch_ends(jax.random.randint(streams_of[4], (N_ROW, N_COL, KMAX), 0, N_ROW * S // TILE), jax.random.fold_in(streams_of[4], 1), 0, (N_ROW * S // TILE) - 1).astype(jnp.int32),
        "tile_count": draw_tile_count(jax.random.fold_in(streams_of[7], 71), 0),
        "cotangent": scatter_about(streams_of[6], (NODES, F), 1.0, 6.0, ((0, 256),)),
    }


def aggregate(slot_tiles, slot_rows, slot_cols, live_count, source, out_tiles, transposed):
    slots = slot_tiles.shape[0]
    tile_size = slot_tiles.shape[1]
    width = source.shape[1]
    blocks = source.reshape(-1, tile_size, width).astype(jnp.float32)
    group_size = 32 if slots % 32 == 0 else slots
    groups = slots // group_size
    active = (jnp.arange(slots).astype(jnp.int32) < live_count).astype(jnp.float32)
    starts = (jnp.arange(groups) * group_size).astype(jnp.int32)

    def accumulate(running, packed):
        tile_group, row_group, col_group, active_group, start = packed

        def work(current):
            tiles_wide = tile_group.astype(jnp.float32)
            if transposed:
                products = jnp.einsum('kab,kaf->kbf', tiles_wide, blocks[row_group])
                placed = col_group
            else:
                products = jnp.einsum('kab,kbf->kaf', tiles_wide, blocks[col_group])
                placed = row_group
            return current.at[placed].add(products * active_group[:, None, None])

        def keep(current):
            return current
        running = lax.cond(start < live_count, work, keep, running)
        return (running, None)
    initial = jnp.zeros((out_tiles, tile_size, width), jnp.float32)
    packed = (slot_tiles.reshape(groups, group_size, tile_size, tile_size), slot_rows.reshape(groups, group_size).astype(jnp.int32), slot_cols.reshape(groups, group_size).astype(jnp.int32), active.reshape(groups, group_size), starts)
    running, _ = lax.scan(accumulate, initial, packed)
    return running.reshape(out_tiles * tile_size, width)

def reference(features, weight, adjacency, tile_row, tile_col, tile_count, cotangent):
    row_devices = N_ROW
    col_devices = N_COL
    cells = row_devices * col_devices
    width = features.shape[1]
    owned = features.shape[0] // cells
    slots = adjacency.shape[2]
    tile_size = adjacency.shape[3]
    flat_tiles = adjacency.reshape(cells, slots, tile_size, tile_size)
    flat_rows = tile_row.reshape(cells, slots)
    flat_cols = tile_col.reshape(cells, slots)
    flat_count = tile_count.reshape(cells)
    row_tiles = col_devices * owned // tile_size
    col_tiles = row_devices * owned // tile_size
    feature_grid = features.reshape(row_devices, col_devices, owned, width)

    def forward_cell(running, cell_index):
        row_index = cell_index // col_devices
        col_index = cell_index % col_devices
        source = lax.dynamic_index_in_dim(feature_grid, col_index, 1, keepdims=False)
        source = source.reshape(row_devices * owned, width)
        partial_value = aggregate(flat_tiles[cell_index], flat_rows[cell_index], flat_cols[cell_index], flat_count[cell_index], source, row_tiles, False)
        running = running.at[row_index].add(partial_value)
        return (running, None)
    initial = jnp.zeros((row_devices, col_devices * owned, width), jnp.float32)
    cell_list = jnp.arange(cells).astype(jnp.int32)
    summed, _ = lax.scan(forward_cell, initial, cell_list)
    aggregated = summed.reshape(-1, width).astype(jnp.bfloat16)
    preact = jnp.dot(aggregated, weight, preferred_element_type=jnp.float32)
    activated, pullback = jax.vjp(jax.nn.gelu, preact)
    output = activated.astype(jnp.bfloat16)
    delta = pullback(cotangent.astype(preact.dtype))[0].astype(jnp.bfloat16)
    grad_weight = jnp.dot(aggregated.T, delta, preferred_element_type=jnp.float32)
    back = jnp.dot(delta, weight.T, preferred_element_type=jnp.float32).astype(jnp.bfloat16)
    back_grid = back.reshape(row_devices, col_devices * owned, width)

    def backward_cell(running, cell_index):
        row_index = cell_index // col_devices
        col_index = cell_index % col_devices
        source = lax.dynamic_index_in_dim(back_grid, row_index, 0, keepdims=False)
        partial_value = aggregate(flat_tiles[cell_index], flat_rows[cell_index], flat_cols[cell_index], flat_count[cell_index], source, col_tiles, True)
        running = running.at[:, col_index].add(partial_value.reshape(row_devices, owned, width))
        return (running, None)
    initial_back = jnp.zeros((row_devices, col_devices, owned, width), jnp.float32)
    spread_back, _ = lax.scan(backward_cell, initial_back, cell_list)
    grad_input = spread_back.reshape(-1, width).astype(jnp.bfloat16)
    return (output, grad_weight, grad_input)
```

```python
import functools
import math

import jax
import jax.numpy as jnp
from jax import lax
from jax.experimental import pallas as pl
from jax.experimental.pallas import tpu as pltpu
from jax.sharding import PartitionSpec as P

MESH = pl.DeviceIdType.MESH
BF16 = jnp.bfloat16
F32 = jnp.float32
TILE = 128
OWNED = 256
WIDTH = 256
NODES = 4096
CHUNK = 16
VMEM_LIMIT = 56 * 1024 * 1024

VMEM_SPEC = pl.BlockSpec(memory_space=pltpu.VMEM)
SMEM_SPEC = pl.BlockSpec(memory_space=pltpu.SMEM)
ANY_SPEC = pl.BlockSpec(memory_space=pl.ANY)


class Place:
    def __init__(self):
        row = lax.axis_index("row")
        col = lax.axis_index("col")
        self.x = row // 4
        self.zl = (row // 2) % 2
        self.core = row % 2
        self.y = col // 4
        self.zh = col % 4

    def at(self, dx=0, dzl=0, dcore=0, dy=0, dzh=0):
        x = (self.x + dx) % 4
        zl = (self.zl + dzl) % 2
        core = (self.core + dcore) % 2
        y = (self.y + dy) % 4
        zh = (self.zh + dzh) % 4
        return (x * 4 + zl * 2 + core, y * 4 + zh)


class Sender:
    def __init__(self, send_sems, recv_sems):
        self.send_sems = send_sems
        self.recv_sems = recv_sems
        self.used = 0
        self.started = []

    def copy(self, src, dst, device):
        made = pltpu.make_async_remote_copy(
            src_ref=src,
            dst_ref=dst,
            send_sem=self.send_sems.at[self.used],
            recv_sem=self.recv_sems.at[self.used],
            device_id=device,
            device_id_type=MESH,
        )
        made.start()
        self.used += 1
        self.started.append(made)
        return made

    def finish(self):
        for made in self.started:
            made.wait_send()


def greet(devices):
    barrier = pltpu.get_barrier_semaphore()
    for device in devices:
        pl.semaphore_signal(barrier, inc=1, device_id=device, device_id_type=MESH)
    pl.semaphore_wait(barrier, len(devices))


def rows_at(start, size):
    return pl.ds(pl.multiple_of(start, TILE), size)


def gather_kernel(features, gathered, send_sems, recv_sems):
    here = Place()
    other = here.at(dcore=1)
    across = here.at(dzl=1)
    right = here.at(dx=1)
    left = here.at(dx=-1)
    greet((other, across, right, left))
    send = Sender(send_sems, recv_sems)

    def block(dx, dzl, part=None):
        row = here.at(dx=dx, dzl=dzl)[0]
        if part is None:
            return gathered.at[rows_at(row * OWNED, OWNED), :]
        return gathered.at[rows_at(row * OWNED + part * TILE, TILE), :]

    def whole(dx, dzl, device):
        return send.copy(block(dx, dzl), block(dx, dzl), device)

    def half(dx, dzl, part, device):
        return send.copy(block(dx, dzl, part), block(dx, dzl, part), device)

    gathered[rows_at(here.at()[0] * OWNED, OWNED), :] = features[...]
    to_across = whole(0, 0, across)
    to_right = [whole(0, 0, right)]
    to_left = [whole(0, 0, left)]
    cores = [whole(0, 0, other)]
    to_across.wait_recv()
    to_right.append(whole(0, 1, right))
    to_left.append(whole(0, 1, left))
    cores.append(whole(0, 1, other))
    far = []
    for dzl in (0, 1):
        to_right[dzl].wait_recv()
        far.append(half(-1, dzl, 0, right))
        cores.append(whole(-1, dzl, other))
        to_left[dzl].wait_recv()
        far.append(half(1, dzl, 1, left))
        cores.append(whole(1, dzl, other))
    for dzl in (0, 1):
        far[2 * dzl].wait_recv()
        far[2 * dzl + 1].wait_recv()
        cores.append(whole(2, dzl, other))
    for made in cores:
        made.wait_recv()
    send.finish()


def gather_features(features):
    return pl.pallas_call(
        gather_kernel,
        out_shape=jax.ShapeDtypeStruct((NODES, WIDTH), BF16),
        in_specs=[VMEM_SPEC],
        out_specs=VMEM_SPEC,
        scratch_shapes=[
            pltpu.SemaphoreType.DMA((24,)),
            pltpu.SemaphoreType.DMA((24,)),
        ],
        compiler_params=pltpu.CompilerParams(
            collective_id=0, has_side_effects=True, vmem_limit_bytes=VMEM_LIMIT
        ),
        name="gather_features",
    )(features)


def product_kernel(transposed, count_ref, row_ref, col_ref, tiles, source, out, held, total, sems):
    live = count_ref[0]
    slots = held.shape[0]
    chunks = slots // CHUNK

    def fetch(chunk):
        part = pl.ds(chunk * CHUNK, CHUNK)
        return pltpu.make_async_copy(tiles.at[part], held.at[part], sems.at[chunk])

    for chunk in range(chunks):
        @pl.when(chunk * CHUNK < live)
        def _():
            fetch(chunk).start()

    total[...] = jnp.zeros_like(total)
    contract = 0 if transposed else 1

    def work(chunk, carry):
        @pl.when(chunk * CHUNK < live)
        def _():
            fetch(chunk).wait()
            for step in range(CHUNK):
                slot = chunk * CHUNK + step
                row = row_ref[slot]
                col = col_ref[slot]
                taken, placed = (row, col) if transposed else (col, row)
                block = source[rows_at(taken * TILE, TILE), :]
                block = jnp.where(slot < live, block, jnp.zeros_like(block))
                product = lax.dot_general(
                    held[slot],
                    block,
                    (((contract,), (0,)), ((), ())),
                    preferred_element_type=F32,
                )
                where = rows_at(placed * TILE, TILE)
                total[where, :] = total[where, :] + product

        return carry

    lax.fori_loop(0, chunks, work, 0)
    out[...] = total[...].astype(BF16)


def products(count, tile_row, tile_col, tiles, source, transposed):
    slots = tiles.shape[0]
    return pl.pallas_call(
        functools.partial(product_kernel, transposed),
        out_shape=jax.ShapeDtypeStruct((NODES, WIDTH), BF16),
        in_specs=[SMEM_SPEC, SMEM_SPEC, SMEM_SPEC, ANY_SPEC, VMEM_SPEC],
        out_specs=VMEM_SPEC,
        scratch_shapes=[
            pltpu.VMEM((slots, TILE, TILE), BF16),
            pltpu.VMEM((NODES, WIDTH), F32),
            pltpu.SemaphoreType.DMA((slots // CHUNK,)),
        ],
        compiler_params=pltpu.CompilerParams(vmem_limit_bytes=VMEM_LIMIT),
        name="products_back" if transposed else "products",
    )(count, tile_row, tile_col, tiles, source)


SLOPE = math.sqrt(2 / math.pi)


def middle_kernel(
    parts, weight, cotangent, output, back_rows, grad_weight,
    from_left, from_right, full_left, full_right, merged_right, merged_left,
    level_send, level_recv, total, term, term_core, term_across, term_x,
    term_y, term_z, chunk_sum, send_sems, recv_sems,
):
    here = Place()
    other = here.at(dcore=1)
    across = here.at(dzl=1)
    ahead = [here.at(dx=step) for step in (1, 2, 3)]
    right = here.at(dy=1)
    left = here.at(dy=-1)
    beside = [here.at(dy=step) for step in (1, 2, 3)]
    levels = [here.at(dzh=step) for step in (2, 1, 3)]
    greet([other, across] + ahead + beside + levels)
    send = Sender(send_sems, recv_sems)
    order = (2, 1, 3, 0)

    def where(dy, dzh, part=None):
        col = here.at(dy=dy, dzh=dzh)[1]
        if part is None:
            return rows_at(col * OWNED, OWNED)
        return rows_at(col * OWNED + part * TILE, TILE)

    first_right, first_left, plain_right, plain_left = {}, {}, {}, {}
    last_right, last_left, to_level = {}, {}, {}

    def first(step):
        dzh = order[step]
        first_right[step] = send.copy(parts.at[where(2, dzh, 0), :], from_left.at[step], right)
        first_left[step] = send.copy(parts.at[where(2, dzh, 1), :], from_right.at[step], left)

    def plain(step):
        dzh = order[step]
        plain_right[step] = send.copy(
            parts.at[where(1, dzh, 1), :], full_left.at[step, pl.ds(TILE, TILE), :], right
        )
        plain_left[step] = send.copy(
            parts.at[where(-1, dzh, 0), :], full_right.at[step, pl.ds(0, TILE), :], left
        )

    def merge(step):
        dzh = order[step]
        first_right[step].wait_recv()
        merged_right[step] = (
            parts[where(1, dzh, 0), :].astype(F32) + from_left[step].astype(F32)
        ).astype(BF16)
        last_right[step] = send.copy(
            merged_right.at[step], full_left.at[step, pl.ds(0, TILE), :], right
        )
        first_left[step].wait_recv()
        merged_left[step] = (
            parts[where(-1, dzh, 1), :].astype(F32) + from_right[step].astype(F32)
        ).astype(BF16)
        last_left[step] = send.copy(
            merged_left.at[step], full_right.at[step, pl.ds(TILE, TILE), :], left
        )

    def complete(step):
        dzh = order[step]
        for made in (plain_right, plain_left, last_right, last_left):
            made[step].wait_recv()
        summed = (
            parts[where(0, dzh), :].astype(F32)
            + full_left[step].astype(F32)
            + full_right[step].astype(F32)
        )
        if step < 3:
            level_send[step] = summed.astype(BF16)
            to_level[step] = send.copy(level_send.at[step], level_recv.at[step], levels[step])
        else:
            total[...] = summed

    first(0)
    plain(0)
    first(1)
    for step in range(4):
        merge(step)
        if step < 2:
            first(step + 2)
        if step < 3:
            plain(step + 1)
        if step:
            complete(step - 1)
    complete(3)
    for step in range(3):
        to_level[step].wait_recv()
    aggregated = (
        total[...]
        + level_recv[0].astype(F32)
        + level_recv[1].astype(F32)
        + level_recv[2].astype(F32)
    ).astype(BF16)

    preact = jnp.dot(aggregated, weight[...], preferred_element_type=F32)
    squared = preact * preact
    bent = jnp.tanh(SLOPE * (preact + 0.044715 * (preact * squared)))
    output[...] = (0.5 * preact * (1.0 + bent)).astype(BF16)
    slope = 0.5 * (1.0 + bent) + 0.5 * preact * (1.0 - bent * bent) * (
        SLOPE * (1.0 + 3 * 0.044715 * squared)
    )
    delta = (cotangent[...].astype(F32) * slope).astype(BF16)
    back = lax.dot_general(
        delta, weight[...], (((1,), (1,)), ((), ())), preferred_element_type=F32
    ).astype(BF16)
    back_rows[where(0, 0), :] = back

    def spread(dy, dzh, device, part=None):
        block = back_rows.at[where(dy, dzh, part), :]
        return send.copy(block, block, device)

    up = [spread(0, 0, levels[1]), spread(0, 0, levels[2]), spread(0, 0, levels[0])]
    came = (3, 1, 2)
    ring_right = [spread(0, 0, right)]
    ring_left = [spread(0, 0, left)]
    halves = []

    def relay(step, dzh):
        ring_right[step].wait_recv()
        halves.append(spread(-1, dzh, right, 0))
        ring_left[step].wait_recv()
        halves.append(spread(1, dzh, left, 1))

    term[...] = lax.dot_general(
        aggregated, delta, (((0,), (0,)), ((), ())), preferred_element_type=F32
    )
    half_mine = here.core * 128
    half_other = 128 - half_mine
    to_core = send.copy(
        term.at[pl.ds(pl.multiple_of(half_other, 128), 128), :], term_core, other
    )

    for step in range(3):
        up[step].wait_recv()
        ring_right.append(spread(0, came[step], right))
        ring_left.append(spread(0, came[step], left))
        if step == 0:
            to_core.wait_recv()
            mine = pl.ds(pl.multiple_of(half_mine, 128), 128)
            term[mine, :] = term[mine, :] + term_core[...]
            quarter_mine = half_mine + here.zl * 64
            quarter_other = half_mine + 64 - here.zl * 64
            to_across = send.copy(
                term.at[pl.ds(pl.multiple_of(quarter_other, 64), 64), :], term_across, across
            )
        if step == 1:
            to_across.wait_recv()
            mine = pl.ds(pl.multiple_of(quarter_mine, 64), 64)
            term[mine, :] = term[mine, :] + term_across[...]
            to_x = []
            for dx in (1, 2, 3):
                piece = quarter_mine + ((here.x + dx) % 4) * 16
                to_x.append(
                    send.copy(
                        term.at[pl.ds(pl.multiple_of(piece, 16), 16), :],
                        term_x.at[dx - 1],
                        ahead[dx - 1],
                    )
                )

    relay(0, 0)
    for made in to_x:
        made.wait_recv()
    piece = pl.ds(pl.multiple_of(quarter_mine + here.x * 16, 16), 16)
    chunk_sum[0] = term[piece, :] + term_x[0] + term_x[1] + term_x[2]
    to_y = [send.copy(chunk_sum.at[0], term_y.at[dy - 1], beside[dy - 1]) for dy in (1, 2, 3)]
    relay(1, came[0])
    for made in to_y:
        made.wait_recv()
    chunk_sum[1] = (chunk_sum[0] + term_y[1]) + (term_y[0] + term_y[2])
    to_z = [send.copy(chunk_sum.at[1], term_z.at[slot], levels[slot]) for slot in range(3)]
    relay(2, came[1])
    for made in to_z:
        made.wait_recv()
    chunk_sum[2] = (chunk_sum[1] + term_z[0]) + (term_z[1] + term_z[2])
    grad_weight[piece, :] = chunk_sum[2]
    all_x = [
        send.copy(grad_weight.at[piece, :], grad_weight.at[piece, :], ahead[dx]) for dx in range(3)
    ]
    relay(3, came[2])
    for made in all_x:
        made.wait_recv()
    quarter = grad_weight.at[pl.ds(pl.multiple_of(quarter_mine, 64), 64), :]
    all_across = send.copy(quarter, quarter, across)
    halves[0].wait_recv()
    halves[1].wait_recv()
    halves[2].wait_recv()
    halves[3].wait_recv()
    all_across.wait_recv()
    half = grad_weight.at[pl.ds(pl.multiple_of(half_mine, 128), 128), :]
    all_core = send.copy(half, half, other)
    for made in halves[4:]:
        made.wait_recv()
    all_core.wait_recv()
    send.finish()


def middle(parts, weight, cotangent):
    block = (TILE, WIDTH)
    full = (OWNED, WIDTH)
    return pl.pallas_call(
        middle_kernel,
        out_shape=(
            jax.ShapeDtypeStruct((OWNED, WIDTH), BF16),
            jax.ShapeDtypeStruct((NODES, WIDTH), BF16),
            jax.ShapeDtypeStruct((WIDTH, WIDTH), F32),
        ),
        in_specs=[VMEM_SPEC] * 3,
        out_specs=(VMEM_SPEC,) * 3,
        scratch_shapes=[
            pltpu.VMEM((4,) + block, BF16),
            pltpu.VMEM((4,) + block, BF16),
            pltpu.VMEM((4,) + full, BF16),
            pltpu.VMEM((4,) + full, BF16),
            pltpu.VMEM((4,) + block, BF16),
            pltpu.VMEM((4,) + block, BF16),
            pltpu.VMEM((3,) + full, BF16),
            pltpu.VMEM((3,) + full, BF16),
            pltpu.VMEM(full, F32),
            pltpu.VMEM((WIDTH, WIDTH), F32),
            pltpu.VMEM((128, WIDTH), F32),
            pltpu.VMEM((64, WIDTH), F32),
            pltpu.VMEM((3, 16, WIDTH), F32),
            pltpu.VMEM((3, 16, WIDTH), F32),
            pltpu.VMEM((3, 16, WIDTH), F32),
            pltpu.VMEM((3, 16, WIDTH), F32),
            pltpu.SemaphoreType.DMA((64,)),
            pltpu.SemaphoreType.DMA((64,)),
        ],
        compiler_params=pltpu.CompilerParams(
            collective_id=1, has_side_effects=True, vmem_limit_bytes=VMEM_LIMIT
        ),
        name="middle",
    )(parts, weight, cotangent)


def scatter_kernel(
    parts, out, core_recv, merged, from_left, from_right, full_left, full_right,
    merged_right, merged_left, level_send, level_recv, send_sems, recv_sems,
):
    here = Place()
    other = here.at(dcore=1)
    across = here.at(dzl=1)
    right = here.at(dx=1)
    left = here.at(dx=-1)
    greet((other, across, right, left))
    send = Sender(send_sems, recv_sems)

    def where(dx, dzl, dcore=0):
        return rows_at(here.at(dx=dx, dzl=dzl, dcore=dcore)[0] * OWNED, OWNED)

    dests = [(dx, dzl) for dzl in (1, 0) for dx in (2, 1, 3, 0)]
    to_core = [
        send.copy(parts.at[where(dx, dzl, 1), :], core_recv.at[slot], other)
        for slot, (dx, dzl) in enumerate(dests)
    ]

    def collect(slot):
        to_core[slot].wait_recv()
        dx, dzl = dests[slot]
        return parts[where(dx, dzl), :].astype(F32) + core_recv[slot].astype(F32)

    low = pl.ds(0, TILE)
    high = pl.ds(TILE, TILE)
    first_right, first_left, plain_right, plain_left = {}, {}, {}, {}
    for step in range(2):
        base = 4 * step
        merged[base] = collect(base).astype(BF16)
        first_right[step] = send.copy(merged.at[base, low, :], from_left.at[step], right)
        first_left[step] = send.copy(merged.at[base, high, :], from_right.at[step], left)
        merged[base + 1] = collect(base + 1).astype(BF16)
        plain_right[step] = send.copy(
            merged.at[base + 1, high, :], full_left.at[step, high, :], right
        )
        merged[base + 2] = collect(base + 2).astype(BF16)
        plain_left[step] = send.copy(merged.at[base + 2, low, :], full_right.at[step, low, :], left)
    last_right, last_left = {}, {}
    for step in range(2):
        base = 4 * step
        first_right[step].wait_recv()
        merged_right[step] = (
            merged[base + 1, low, :].astype(F32) + from_left[step].astype(F32)
        ).astype(BF16)
        last_right[step] = send.copy(merged_right.at[step], full_left.at[step, low, :], right)
        first_left[step].wait_recv()
        merged_left[step] = (
            merged[base + 2, high, :].astype(F32) + from_right[step].astype(F32)
        ).astype(BF16)
        last_left[step] = send.copy(merged_left.at[step], full_right.at[step, high, :], left)
    for step in range(2):
        own = collect(4 * step + 3)
        for made in (plain_right, plain_left, last_right, last_left):
            made[step].wait_recv()
        summed = own + full_left[step].astype(F32) + full_right[step].astype(F32)
        if step == 0:
            level_send[...] = summed.astype(BF16)
            to_across = send.copy(level_send, level_recv, across)
        else:
            to_across.wait_recv()
            out[...] = (summed + level_recv[...].astype(F32)).astype(BF16)
    send.finish()


def scatter(parts):
    block = (TILE, WIDTH)
    full = (OWNED, WIDTH)
    return pl.pallas_call(
        scatter_kernel,
        out_shape=jax.ShapeDtypeStruct(full, BF16),
        in_specs=[VMEM_SPEC],
        out_specs=VMEM_SPEC,
        scratch_shapes=[
            pltpu.VMEM((8,) + full, BF16),
            pltpu.VMEM((8,) + full, BF16),
            pltpu.VMEM((2,) + block, BF16),
            pltpu.VMEM((2,) + block, BF16),
            pltpu.VMEM((2,) + full, BF16),
            pltpu.VMEM((2,) + full, BF16),
            pltpu.VMEM((2,) + block, BF16),
            pltpu.VMEM((2,) + block, BF16),
            pltpu.VMEM(full, BF16),
            pltpu.VMEM(full, BF16),
            pltpu.SemaphoreType.DMA((24,)),
            pltpu.SemaphoreType.DMA((24,)),
        ],
        compiler_params=pltpu.CompilerParams(
            collective_id=2, has_side_effects=True, vmem_limit_bytes=VMEM_LIMIT
        ),
        name="scatter",
    )(parts)


def shards(features, weight, adjacency, tile_row, tile_col, tile_count, cotangent):
    tiles = adjacency[0, 0]
    slot_rows = tile_row[0, 0]
    slot_cols = tile_col[0, 0]
    count = tile_count[0]
    source = gather_features(features)
    parts = products(count, slot_rows, slot_cols, tiles, source, False)
    output, back_rows, grad_weight = middle(parts, weight, cotangent)
    parts_back = products(count, slot_rows, slot_cols, tiles, back_rows, True)
    grad_input = scatter(parts_back)
    return output, grad_weight, grad_input


def solution(mesh):
    return jax.shard_map(
        shards,
        mesh=mesh,
        in_specs=(
            P(("row", "col"), None),
            P(),
            P("row", "col", None, None, None),
            P("row", "col", None),
            P("row", "col", None),
            P("row", "col"),
            P(("row", "col"), None),
        ),
        out_specs=(P(("row", "col"), None), P(), P(("row", "col"), None)),
        check_vma=False,
    )
```

```python
import functools
import math

import jax
import jax.numpy as jnp
from jax import lax
from jax.experimental import pallas as pl
from jax.experimental.pallas import tpu as pltpu
from jax.sharding import PartitionSpec as P

MESH = pl.DeviceIdType.MESH
BF16 = jnp.bfloat16
F32 = jnp.float32
TILE = 128
OWNED = 256
WIDTH = 256
HALF = 128
NODES = 4096
TILES = NODES // TILE
GROUP = 16
COPIES = 256
VMEM_LIMIT = 58 * 1024 * 1024
SLOPE = math.sqrt(2 / math.pi)

VMEM_SPEC = pl.BlockSpec(memory_space=pltpu.VMEM)
SMEM_SPEC = pl.BlockSpec(memory_space=pltpu.SMEM)
ANY_SPEC = pl.BlockSpec(memory_space=pl.ANY)
LOW = pl.ds(0, TILE)
HIGH = pl.ds(TILE, TILE)


def arrange(placed, taken, live):
    slots = placed.shape[1]
    lane = lax.broadcasted_iota(jnp.int32, (slots, slots), 1)
    line = lax.broadcasted_iota(jnp.int32, (slots, slots), 0)

    def turned(flat):
        return jnp.sum(jnp.where(lane == line, flat, 0), axis=1, keepdims=True)

    lane_row = lax.broadcasted_iota(jnp.int32, (1, slots), 1)
    tagged = jnp.where(lane_row < live, placed, TILES)
    key = tagged * 256 + lane_row
    rank = jnp.sum(jnp.where(key < turned(key), 1, 0), axis=1, keepdims=True)
    tag_line = turned(tagged)
    taken_line = turned(taken)
    chosen = rank == lane

    def pick(column):
        return jnp.sum(jnp.where(chosen, column, 0), axis=0, keepdims=True)

    order = pick(line)
    source = pick(taken_line)
    tag = pick(tag_line + 1)
    before = jnp.sum(jnp.where(rank + 1 == lane, tag_line + 1, 0), axis=0, keepdims=True)
    keep = jnp.where(tag == before, 1, 0)
    up_to = jnp.sum(jnp.where(tag_line <= lane, 1, 0), axis=0, keepdims=True)
    here = jnp.sum(jnp.where(tag_line == lane, 1, 0), axis=0, keepdims=True)
    last = jnp.where(here > 0, up_to - 1, slots)
    return (order, source, keep, last)


def order_kernel(count_ref, row_ref, col_ref, out):
    live = count_ref[0]
    rows = row_ref[...]
    cols = col_ref[...]
    found = arrange(rows, cols, live) + arrange(cols, rows, live)
    for line, value in enumerate(found):
        out[line : line + 1, :] = value


def order_slots(count, tile_row, tile_col):
    slots = tile_row.shape[1]
    return pl.pallas_call(
        order_kernel,
        out_shape=jax.ShapeDtypeStruct((8, slots), jnp.int32),
        in_specs=[SMEM_SPEC, VMEM_SPEC, VMEM_SPEC],
        out_specs=VMEM_SPEC,
        name="order_slots",
    )(count, tile_row, tile_col)


class Place:
    def __init__(self):
        row = lax.axis_index("row")
        col = lax.axis_index("col")
        self.x = row // 4
        self.zl = (row // 2) % 2
        self.core = row % 2
        self.y = col // 4
        self.zh = col % 4

    def at(self, dx=0, dzl=0, dcore=0, dy=0, dzh=0):
        x = (self.x + dx) % 4
        zl = (self.zl + dzl) % 2
        core = (self.core + dcore) % 2
        y = (self.y + dy) % 4
        zh = (self.zh + dzh) % 4
        return (x * 4 + zl * 2 + core, y * 4 + zh)


class Copy:
    def __init__(self, describe):
        self.describe = describe

    def wait_recv(self):
        self.describe().wait_recv()

    def wait_send(self):
        self.describe().wait_send()


class Sender:
    def __init__(self, send_sems, recv_sems):
        self.send_sems = send_sems
        self.recv_sems = recv_sems
        self.started = []

    def copy(self, ends, device):
        used = len(self.started)

        def describe():
            src, dst = ends()
            return pltpu.make_async_remote_copy(
                src_ref=src,
                dst_ref=dst,
                send_sem=self.send_sems.at[used],
                recv_sem=self.recv_sems.at[used],
                device_id=device,
                device_id_type=MESH,
            )

        describe().start()
        made = Copy(describe)
        self.started.append(made)
        return made

    def finish(self):
        for made in self.started:
            made.wait_send()


def greet(devices):
    barrier = pltpu.get_barrier_semaphore()
    for device in devices:
        pl.semaphore_signal(barrier, inc=1, device_id=device, device_id_type=MESH)
    pl.semaphore_wait(barrier, len(devices))


def rows_at(start, size):
    return pl.ds(pl.multiple_of(start, TILE), size)


class Around:
    def __init__(self, here):
        self.here = here
        self.other = here.at(dcore=1)
        self.across = here.at(dzl=1)
        self.ahead = [here.at(dx=step) for step in (1, 2, 3)]
        self.beside = [here.at(dy=step) for step in (1, 2, 3)]
        self.levels = [here.at(dzh=step) for step in (2, 1, 3)]

    def everyone(self):
        return [self.other, self.across] + self.ahead + self.beside + self.levels


def gather_steps(around, send, gathered):
    here = around.here
    right, left = around.ahead[0], around.ahead[2]
    to_right, to_left, cores, far = [], [], [], []
    state = {}

    def block(dx, dzl, part=None):
        row = here.at(dx=dx, dzl=dzl)[0]
        if part is None:
            return gathered.at[pl.ds(row * 2, 2)]
        return gathered.at[row * 2 + part]

    def move(dx, dzl, device, part=None):
        return send.copy(lambda dx=dx, dzl=dzl: (block(dx, dzl, part), block(dx, dzl, part)), device)

    def begin():
        state["across"] = move(0, 0, around.across)
        to_right.append(move(0, 0, right))
        to_left.append(move(0, 0, left))
        cores.append(move(0, 0, around.other))

    def second():
        state["across"].wait_recv()
        to_right.append(move(0, 1, right))
        to_left.append(move(0, 1, left))
        cores.append(move(0, 1, around.other))

    def relay(dzl):
        to_right[dzl].wait_recv()
        far.append(move(-1, dzl, right, 0))
        cores.append(move(-1, dzl, around.other))
        to_left[dzl].wait_recv()
        far.append(move(1, dzl, left, 1))
        cores.append(move(1, dzl, around.other))

    def last(dzl):
        far[2 * dzl].wait_recv()
        far[2 * dzl + 1].wait_recv()
        cores.append(move(2, dzl, around.other))

    def end():
        for made in cores:
            made.wait_recv()

    return [
        begin,
        second,
        functools.partial(relay, 0),
        functools.partial(relay, 1),
        functools.partial(last, 0),
        functools.partial(last, 1),
        end,
    ]


def reduce_steps(
    around, send, parts, from_left, from_right, full_left, full_right,
    merged_right, merged_left, level_send, level_recv, total, result,
):
    here = around.here
    right, left = around.beside[0], around.beside[2]
    order = (2, 1, 3, 0)
    first_right, first_left, plain_right, plain_left = {}, {}, {}, {}
    last_right, last_left, to_level = {}, {}, {}

    def where(dy, dzh, part=None):
        col = here.at(dy=dy, dzh=dzh)[1]
        if part is None:
            return rows_at(col * OWNED, OWNED)
        return rows_at(col * OWNED + part * TILE, TILE)

    def first(step):
        dzh = order[step]
        first_right[step] = send.copy(lambda step=step, dzh=dzh: (parts.at[where(2, dzh, 0), :], from_left.at[step]), right)
        first_left[step] = send.copy(lambda step=step, dzh=dzh: (parts.at[where(2, dzh, 1), :], from_right.at[step]), left)

    def plain(step):
        dzh = order[step]
        plain_right[step] = send.copy(lambda step=step, dzh=dzh: (parts.at[where(1, dzh, 1), :], full_left.at[step, HIGH, :]), right)
        plain_left[step] = send.copy(lambda step=step, dzh=dzh: (parts.at[where(-1, dzh, 0), :], full_right.at[step, LOW, :]), left)

    def merge(step):
        dzh = order[step]
        first_right[step].wait_recv()
        merged_right[step] = (
            parts[where(1, dzh, 0), :].astype(F32) + from_left[step].astype(F32)
        ).astype(BF16)
        last_right[step] = send.copy(lambda step=step: (merged_right.at[step], full_left.at[step, LOW, :]), right)
        first_left[step].wait_recv()
        merged_left[step] = (
            parts[where(-1, dzh, 1), :].astype(F32) + from_right[step].astype(F32)
        ).astype(BF16)
        last_left[step] = send.copy(lambda step=step: (merged_left.at[step], full_right.at[step, HIGH, :]), left)

    def complete(step):
        dzh = order[step]
        for made in (plain_right, plain_left, last_right, last_left):
            made[step].wait_recv()
        summed = (
            parts[where(0, dzh), :].astype(F32)
            + full_left[step].astype(F32)
            + full_right[step].astype(F32)
        )
        if step < 3:
            level_send[step] = summed.astype(BF16)
            to_level[step] = send.copy(lambda step=step: (level_send.at[step], level_recv.at[step]), around.levels[step])
        else:
            total[...] = summed

    def begin():
        first(0)
        plain(0)
        first(1)

    def middle(step):
        merge(step)
        if step < 2:
            first(step + 2)
        if step < 3:
            plain(step + 1)
        if step:
            complete(step - 1)

    def end():
        for step in range(3):
            to_level[step].wait_recv()
        result[...] = (
            total[...]
            + level_recv[0].astype(F32)
            + level_recv[1].astype(F32)
            + level_recv[2].astype(F32)
        ).astype(BF16)

    return (
        [begin]
        + [functools.partial(middle, step) for step in range(4)]
        + [functools.partial(complete, 3), end]
    )


def spread_steps(around, send, gathered):
    here = around.here
    right, left = around.beside[0], around.beside[2]
    ring_right, ring_left, halves = [], [], []
    up = {}
    came = {1: 3, 2: 1, 0: 2}
    rounds = [0, 3, 1, 2]

    def block(dy, dzh, part):
        col = here.at(dy=dy, dzh=dzh)[1]
        if part is None:
            return gathered.at[pl.ds(col * 2, 2)]
        return gathered.at[col * 2 + part]

    def move(dy, dzh, device, part=None):
        return send.copy(lambda: (block(dy, dzh, part), block(dy, dzh, part)), device)

    def ring(dzh):
        ring_right.append(move(0, dzh, right))
        ring_left.append(move(0, dzh, left))

    def begin():
        up[1] = move(0, 0, around.levels[1])
        up[2] = move(0, 0, around.levels[2])
        ring(0)

    def far():
        up[0] = move(0, 0, around.levels[0])

    def level(slot):
        up[slot].wait_recv()
        ring(came[slot])

    def relay(step):
        dzh = rounds[step]
        ring_right[step].wait_recv()
        halves.append(move(-1, dzh, right, 0))
        ring_left[step].wait_recv()
        halves.append(move(1, dzh, left, 1))

    def end():
        for made in halves:
            made.wait_recv()

    return {
        "begin": begin,
        "far": far,
        "level1": functools.partial(level, 1),
        "level2": functools.partial(level, 2),
        "level0": functools.partial(level, 0),
        "relay0": functools.partial(relay, 0),
        "relay1": functools.partial(relay, 1),
        "relay2": functools.partial(relay, 2),
        "relay3": functools.partial(relay, 3),
        "end": end,
    }


def scatter_steps(
    around, send, parts, out, core_recv, merged, from_left, from_right,
    full_left, full_right, merged_right, merged_left, level_send, level_recv,
):
    here = around.here
    right, left = around.ahead[0], around.ahead[2]
    dests = [(dx, dzl) for dzl in (1, 0) for dx in (2, 1, 3, 0)]
    to_core = []
    first_right, first_left, plain_right, plain_left = {}, {}, {}, {}
    last_right, last_left, state = {}, {}, {}

    def where(dx, dzl, dcore=0):
        return rows_at(here.at(dx=dx, dzl=dzl, dcore=dcore)[0] * OWNED, OWNED)

    def begin():
        for slot, (dx, dzl) in enumerate(dests):
            to_core.append(
                send.copy(lambda slot=slot, dx=dx, dzl=dzl: (parts.at[where(dx, dzl, 1), :], core_recv.at[slot]), around.other)
            )

    def collect(slot):
        to_core[slot].wait_recv()
        dx, dzl = dests[slot]
        return parts[where(dx, dzl), :].astype(F32) + core_recv[slot].astype(F32)

    def first(step):
        base = 4 * step
        merged[base] = collect(base).astype(BF16)
        first_right[step] = send.copy(lambda step=step: (merged.at[base, LOW, :], from_left.at[step]), right)
        first_left[step] = send.copy(lambda step=step: (merged.at[base, HIGH, :], from_right.at[step]), left)
        merged[base + 1] = collect(base + 1).astype(BF16)
        plain_right[step] = send.copy(lambda step=step: (merged.at[base + 1, HIGH, :], full_left.at[step, HIGH, :]), right)
        merged[base + 2] = collect(base + 2).astype(BF16)
        plain_left[step] = send.copy(lambda step=step: (merged.at[base + 2, LOW, :], full_right.at[step, LOW, :]), left)

    def last(step):
        base = 4 * step
        first_right[step].wait_recv()
        merged_right[step] = (
            merged[base + 1, LOW, :].astype(F32) + from_left[step].astype(F32)
        ).astype(BF16)
        last_right[step] = send.copy(lambda step=step: (merged_right.at[step], full_left.at[step, LOW, :]), right)
        first_left[step].wait_recv()
        merged_left[step] = (
            merged[base + 2, HIGH, :].astype(F32) + from_right[step].astype(F32)
        ).astype(BF16)
        last_left[step] = send.copy(lambda step=step: (merged_left.at[step], full_right.at[step, HIGH, :]), left)

    def complete(step):
        own = collect(4 * step + 3)
        for made in (plain_right, plain_left, last_right, last_left):
            made[step].wait_recv()
        summed = own + full_left[step].astype(F32) + full_right[step].astype(F32)
        if step == 0:
            level_send[...] = summed.astype(BF16)
            state["across"] = send.copy(lambda: (level_send, level_recv), around.across)
        else:
            state["across"].wait_recv()
            out[...] = (summed + level_recv[...].astype(F32)).astype(BF16)

    return [begin] + [
        functools.partial(step, number) for step in (first, last, complete) for number in (0, 1)
    ]


def weight_steps(
    around, send, term, grad_weight, term_core, term_across, term_x, term_y, term_z, chunk_sum
):
    here = around.here
    half_mine = here.core * 128
    half_other = 128 - half_mine
    quarter_mine = half_mine + here.zl * 64
    quarter_other = half_mine + 64 - here.zl * 64
    piece_mine = quarter_mine + here.x * 16
    state = {}

    def lines(start, size):
        return pl.ds(pl.multiple_of(start, size), size)

    def same(start, size, device):
        def ends():
            block = grad_weight.at[lines(start, size), :]
            return block, block

        return send.copy(ends, device)

    def core():
        state["core"] = send.copy(lambda: (term.at[lines(half_other, 128), :], term_core), around.other)

    def across():
        state["core"].wait_recv()
        mine = lines(half_mine, 128)
        term[mine, :] = term[mine, :] + term_core[...]
        state["across"] = send.copy(lambda: (term.at[lines(quarter_other, 64), :], term_across), around.across)

    def along():
        state["across"].wait_recv()
        mine = lines(quarter_mine, 64)
        term[mine, :] = term[mine, :] + term_across[...]
        state["x"] = [
            send.copy(lambda dx=dx: (term.at[lines(quarter_mine + ((here.x + dx) % 4) * 16, 16), :], term_x.at[dx - 1]), around.ahead[dx - 1])
            for dx in (1, 2, 3)
        ]

    def over_y():
        for made in state["x"]:
            made.wait_recv()
        chunk_sum[0] = term[lines(piece_mine, 16), :] + term_x[0] + term_x[1] + term_x[2]
        state["y"] = [
            send.copy(lambda slot=slot: (chunk_sum.at[0], term_y.at[slot]), around.beside[slot]) for slot in range(3)
        ]

    def over_z():
        for made in state["y"]:
            made.wait_recv()
        chunk_sum[1] = (chunk_sum[0] + term_y[1]) + (term_y[0] + term_y[2])
        state["z"] = [
            send.copy(lambda slot=slot: (chunk_sum.at[1], term_z.at[slot]), around.levels[slot]) for slot in range(3)
        ]

    def whole_x():
        for made in state["z"]:
            made.wait_recv()
        piece = lines(piece_mine, 16)
        grad_weight[piece, :] = (chunk_sum[1] + term_z[0]) + (term_z[1] + term_z[2])
        state["all_x"] = [same(piece_mine, 16, around.ahead[slot]) for slot in range(3)]

    def whole_across():
        for made in state["all_x"]:
            made.wait_recv()
        state["all_across"] = same(quarter_mine, 64, around.across)

    def whole_core():
        state["all_across"].wait_recv()
        state["all_core"] = same(half_mine, 128, around.other)

    def end():
        state["all_core"].wait_recv()

    return [core, across, along, over_y, over_z, whole_x, whole_across, whole_core, end]


def layer_kernel(plan, features, weight, cotangent, tiles, output, grad_weight, grad_input, *rest):
    (
        sources, backs, parts, parts_back, held, prefix, running,
        from_left, from_right, full_left, full_right, merged_right, merged_left,
        level_send, level_recv, total, aggregated,
        core_recv, merged, x_from_left, x_from_right, x_full_left, x_full_right,
        x_merged_right, x_merged_left, x_level_send, x_level_recv, result,
        term, term_core, term_across, term_x, term_y, term_z, chunk_sum,
        tile_sem, send_sems, recv_sems,
    ) = rest
    slots = held.shape[0]
    prefix[slots] = jnp.zeros((TILE, HALF), BF16)
    load = pltpu.make_async_copy(tiles, held, tile_sem)
    load.start()
    around = Around(Place())
    here = around.here
    greet(around.everyone())
    send = Sender(send_sems, recv_sems)
    columns = [pl.ds(half * HALF, HALF) for half in range(2)]

    def product(line, transposed, half, source, placed, services):
        contract = 0 if transposed else 1
        running[...] = jnp.zeros_like(running)

        def group(number, carry):
            for at, steps in services:
                @pl.when(number == at)
                def _():
                    for step in steps:
                        step()

            for step in range(GROUP):
                slot = number * GROUP + step
                block = source[plan[line + 1, slot]]
                fresh = lax.dot_general(
                    held[plan[line, slot]],
                    block,
                    (((contract,), (0,)), ((), ())),
                    preferred_element_type=F32,
                )
                running[...] = fresh + plan[line + 2, slot].astype(F32) * running[...]
                prefix[slot] = running[...].astype(BF16)
            return carry

        lax.fori_loop(0, slots // GROUP, group, 0)

        def place(tile, carry):
            placed[rows_at(tile * TILE, TILE), :] = prefix[plan[line + 3, tile]]
            return carry

        lax.fori_loop(0, TILES, place, 0, unroll=4)

    mine = here.at()[0] * 2
    gathers = []
    for half in range(2):
        for part in range(2):
            sources[half][mine + part] = features[pl.ds(part * TILE, TILE), columns[half]]
        gathers.append(gather_steps(around, send, sources[half]))
    one, two = gathers
    one[0]()
    one[1]()
    two[0]()
    one[2]()
    two[1]()
    one[3]()
    two[2]()
    one[4]()
    one[5]()
    two[3]()
    one[6]()
    load.wait()
    product(0, False, 0, sources[0], parts[0], [(4, two[4:6])])
    two[6]()

    reduces = [
        reduce_steps(
            around, send, parts[half], from_left.at[half], from_right.at[half],
            full_left.at[half], full_right.at[half], merged_right.at[half],
            merged_left.at[half], level_send.at[half], level_recv.at[half],
            total.at[half], aggregated.at[half],
        )
        for half in range(2)
    ]
    one, two = reduces
    one[0]()
    product(0, False, 1, sources[1], parts[1], [(4, one[1:2]), (9, one[2:3])])
    two[0]()
    one[3]()
    two[1]()
    one[4]()
    two[2]()
    one[5]()
    two[3]()
    one[6]()
    two[4]()
    two[5]()
    two[6]()

    gathered = jnp.concatenate([aggregated[0], aggregated[1]], axis=1)
    preact = jnp.dot(gathered, weight[...], preferred_element_type=F32)
    squared = preact * preact
    bent = jnp.tanh(SLOPE * (preact + 0.044715 * (preact * squared)))
    output[...] = (0.5 * preact * (1.0 + bent)).astype(BF16)
    slope = 0.5 * (1.0 + bent) + 0.5 * preact * (1.0 - bent * bent) * (
        SLOPE * (1.0 + 3 * 0.044715 * squared)
    )
    delta = (cotangent[...].astype(F32) * slope).astype(BF16)
    back = lax.dot_general(
        delta, weight[...], (((1,), (1,)), ((), ())), preferred_element_type=F32
    ).astype(BF16)
    mine = here.at()[1] * 2
    spreads = []
    for half in range(2):
        for part in range(2):
            backs[half][mine + part] = back[
                part * TILE : (part + 1) * TILE, half * HALF : (half + 1) * HALF
            ]
        spreads.append(spread_steps(around, send, backs[half]))
    one, two = spreads
    one["begin"]()
    term[...] = lax.dot_general(
        gathered, delta, (((0,), (0,)), ((), ())), preferred_element_type=F32
    )
    weights = weight_steps(
        around, send, term, grad_weight, term_core, term_across, term_x, term_y, term_z, chunk_sum
    )
    weights[0]()
    one["level1"]()
    one["far"]()
    one["level2"]()
    two["begin"]()
    one["relay0"]()
    weights[1]()
    one["relay1"]()
    one["level0"]()
    weights[2]()
    two["level1"]()
    two["far"]()
    one["relay2"]()
    two["level2"]()
    two["relay0"]()
    one["relay3"]()
    weights[3]()
    two["level0"]()
    one["end"]()
    product(
        4, True, 0, backs[0], parts_back[0],
        [(2, [two["relay1"]]), (6, [two["relay2"], weights[4]]), (10, [two["relay3"]])],
    )
    scatters = [
        scatter_steps(
            around, send, parts_back[half], result.at[half], core_recv.at[half],
            merged.at[half], x_from_left.at[half], x_from_right.at[half],
            x_full_left.at[half], x_full_right.at[half], x_merged_right.at[half],
            x_merged_left.at[half], x_level_send.at[half], x_level_recv.at[half],
        )
        for half in range(2)
    ]
    one_x, two_x = scatters
    one_x[0]()
    two["end"]()
    weights[5]()
    product(
        4, True, 1, backs[1], parts_back[1],
        [(2, one_x[1:3]), (6, one_x[3:4] + weights[6:7]), (9, one_x[4:5] + weights[7:8])],
    )
    two_x[0]()
    one_x[5]()
    two_x[1]()
    two_x[2]()
    one_x[6]()
    two_x[3]()
    two_x[4]()
    weights[8]()
    two_x[5]()
    two_x[6]()
    for half in range(2):
        grad_input[:, columns[half]] = result[half]
    send.finish()


def layer(plan, features, weight, cotangent, tiles):
    slots = tiles.shape[0]
    block = (TILE, HALF)
    full = (OWNED, HALF)
    nodes = pltpu.VMEM((NODES, HALF), BF16)
    stacked = pltpu.VMEM((TILES, TILE, HALF), BF16)

    def pair(lead, shape):
        return pltpu.VMEM((2, lead) + shape, BF16)

    return pl.pallas_call(
        layer_kernel,
        out_shape=(
            jax.ShapeDtypeStruct((OWNED, WIDTH), BF16),
            jax.ShapeDtypeStruct((WIDTH, WIDTH), F32),
            jax.ShapeDtypeStruct((OWNED, WIDTH), BF16),
        ),
        in_specs=[SMEM_SPEC, VMEM_SPEC, VMEM_SPEC, VMEM_SPEC, ANY_SPEC],
        out_specs=(VMEM_SPEC,) * 3,
        scratch_shapes=[
            [stacked, stacked],
            [stacked, stacked],
            [nodes, nodes],
            [nodes, nodes],
            pltpu.VMEM((slots, TILE, TILE), BF16),
            pltpu.VMEM((slots + 1,) + block, BF16),
            pltpu.VMEM(block, F32),
            pair(4, block),
            pair(4, block),
            pair(4, full),
            pair(4, full),
            pair(4, block),
            pair(4, block),
            pair(3, full),
            pair(3, full),
            pltpu.VMEM((2,) + full, F32),
            pltpu.VMEM((2,) + full, BF16),
            pair(8, full),
            pair(8, full),
            pair(2, block),
            pair(2, block),
            pair(2, full),
            pair(2, full),
            pair(2, block),
            pair(2, block),
            pltpu.VMEM((2,) + full, BF16),
            pltpu.VMEM((2,) + full, BF16),
            pltpu.VMEM((2,) + full, BF16),
            pltpu.VMEM((WIDTH, WIDTH), F32),
            pltpu.VMEM((128, WIDTH), F32),
            pltpu.VMEM((64, WIDTH), F32),
            pltpu.VMEM((3, 16, WIDTH), F32),
            pltpu.VMEM((3, 16, WIDTH), F32),
            pltpu.VMEM((3, 16, WIDTH), F32),
            pltpu.VMEM((2, 16, WIDTH), F32),
            pltpu.SemaphoreType.DMA,
            pltpu.SemaphoreType.DMA((COPIES,)),
            pltpu.SemaphoreType.DMA((COPIES,)),
        ],
        compiler_params=pltpu.CompilerParams(
            collective_id=0, has_side_effects=True, vmem_limit_bytes=VMEM_LIMIT
        ),
        name="layer",
    )(plan, features, weight, cotangent, tiles)


def shards(features, weight, adjacency, tile_row, tile_col, tile_count, cotangent):
    plan = order_slots(tile_count[0], tile_row[0], tile_col[0])
    return layer(plan, features, weight, cotangent, adjacency[0, 0])


def solution(mesh):
    return jax.shard_map(
        shards,
        mesh=mesh,
        in_specs=(
            P(("row", "col"), None),
            P(),
            P("row", "col", None, None, None),
            P("row", "col", None),
            P("row", "col", None),
            P("row", "col"),
            P(("row", "col"), None),
        ),
        out_specs=(P(("row", "col"), None), P(), P(("row", "col"), None)),
        check_vma=False,
    )
```

```python
import functools
import math

import jax
import jax.numpy as jnp
from jax import lax
from jax.experimental import pallas as pl
from jax.experimental.pallas import tpu as pltpu
from jax.sharding import PartitionSpec as P

MESH = pl.DeviceIdType.MESH
BF16 = jnp.bfloat16
F32 = jnp.float32
TILE = 128
OWNED = 256
WIDTH = 256
HALF = 128
NODES = 4096
TILES = NODES // TILE
GROUP = 32
COPIES = 128
LOADS = 4
GATHER_BEGIN = ("g0.own", "g1.own",)
GATHER_FIRST = ("g0.core0", "g0.core1", "g0.core3", "g0.core2", "g0.end",)
GATHER_DURING = ((2, ("g1.core0", "g1.core1",)), (4, ("g1.core3", "g1.core2",)))
GATHER_LAST = ("g1.end",)
REDUCE_FIRST = ("r0.first0", "r0.first1", "r0.plain",)
REDUCE_DURING = ((5, ("r0.merge",)),)
REDUCE_LAST = ("r0.late", "r0.last", "r1.first0", "r1.first1", "r1.plain", "r0.sum2", "r0.sum3", "r0.sum1", "r0.sum0", "r1.merge", "r1.late", "r1.last", "r0.end", "r1.sum2", "r1.sum3", "r1.sum1", "r1.sum0", "r1.end",)
SPREAD_BEGIN = ("s0.begin", "s0.far", "s1.begin", "s1.far",)
SPREAD_FIRST = ("w.weight0", "s0.relay0", "s1.relay0", "s0.level1", "s0.level2", "s0.level0", "s0.relay3", "s0.relay1", "w.weight1", "s1.level1", "s1.level2", "s1.level0", "w.weight2", "s0.end",)
SPREAD_DURING = ((1, ("s1.relay3",)), (3, ("s1.relay1", "w.weight3",)))
SPREAD_LAST = ("c0.cores", "s1.end", "w.weight4",)
SCATTER_DURING = ((2, ("c0.chips0",)), (3, ("c0.chips1", "w.weight5",)), (5, ("w.weight6",)))
SCATTER_LAST = ("c1.cores", "w.weight7", "c1.chips0", "c1.chips1", "w.weight8", "c0.end", "c1.end",)
VMEM_LIMIT = 58 * 1024 * 1024
SLOPE = math.sqrt(2 / math.pi)

VMEM_SPEC = pl.BlockSpec(memory_space=pltpu.VMEM)
SMEM_SPEC = pl.BlockSpec(memory_space=pltpu.SMEM)
ANY_SPEC = pl.BlockSpec(memory_space=pl.ANY)
LOW = pl.ds(0, TILE)
HIGH = pl.ds(TILE, TILE)


def gather_place(tile):
    return (tile & 2) * 8 + (tile >> 3) * 4 + ((tile >> 2) & 1) * 2 + (tile & 1)


def scatter_place(tile):
    return (tile & 2) * 8 + ((tile >> 2) & 1) * 8 + (tile >> 3) * 2 + (tile & 1)


def arrange(placed, taken, live):
    slots = placed.shape[1]
    lane = lax.broadcasted_iota(jnp.int32, (slots, slots), 1)
    line = lax.broadcasted_iota(jnp.int32, (slots, slots), 0)

    def turned(flat):
        return jnp.sum(jnp.where(lane == line, flat, 0), axis=1, keepdims=True)

    lane_row = lax.broadcasted_iota(jnp.int32, (1, slots), 1)
    tagged = jnp.where(lane_row < live, placed, TILES)
    key = tagged * 256 + lane_row
    rank = jnp.sum(jnp.where(key < turned(key), 1, 0), axis=1, keepdims=True)
    tag_line = turned(tagged)
    taken_line = turned(taken)
    chosen = rank == lane

    def pick(column):
        return jnp.sum(jnp.where(chosen, column, 0), axis=0, keepdims=True)

    order = pick(line)
    source = pick(taken_line)
    tag = pick(tag_line + 1)
    before = jnp.sum(jnp.where(rank + 1 == lane, tag_line + 1, 0), axis=0, keepdims=True)
    keep = jnp.where(tag == before, 1, 0)
    up_to = jnp.sum(jnp.where(tag_line <= lane, 1, 0), axis=0, keepdims=True)
    here = jnp.sum(jnp.where(tag_line == lane, 1, 0), axis=0, keepdims=True)
    last = jnp.where(here > 0, up_to - 1, slots)
    return (order, source, keep, last)


class Place:
    def __init__(self):
        row = lax.axis_index("row")
        col = lax.axis_index("col")
        four, two = jnp.int32(4), jnp.int32(2)
        self.x = lax.div(row, four)
        self.zl = lax.rem(lax.div(row, two), two)
        self.core = lax.rem(row, two)
        self.y = lax.div(col, four)
        self.zh = lax.rem(col, four)
        xs = [lax.rem(self.x + step, four) * 4 for step in range(4)]
        zls = [self.zl * 2, 2 - self.zl * 2]
        cores = [self.core, 1 - self.core]
        ys = [lax.rem(self.y + step, four) * 4 for step in range(4)]
        zhs = [lax.rem(self.zh + step, four) for step in range(4)]
        self.rows = [[[x + zl + core for core in cores] for zl in zls] for x in xs]
        self.gather_tiles = [[cores[0] * 16 + x + zl for zl in zls] for x in xs]
        self.gather_pairs = [cores[0] * 16 + x for x in xs]
        self.scatter_groups = [[core * 16 + zl * 4 for zl in zls] for core in cores]
        self.scatter_spots = [lax.rem(self.x + step, four) * 2 for step in range(4)]
        self.cols = [[y + zh for zh in zhs] for y in ys]

    def at(self, dx=0, dzl=0, dcore=0, dy=0, dzh=0):
        return (self.rows[dx % 4][dzl % 2][dcore % 2], self.cols[dy % 4][dzh % 4])


class Copy:
    def __init__(self, describe):
        self.describe = describe

    def wait_recv(self):
        self.describe().wait_recv()

    def wait_send(self):
        self.describe().wait_send()


class Sender:
    def __init__(self, send_sems, recv_sems):
        self.send_sems = send_sems
        self.recv_sems = recv_sems
        self.started = []

    def copy(self, ends, device):
        used = len(self.started)

        def describe():
            src, dst = ends()
            return pltpu.make_async_remote_copy(
                src_ref=src,
                dst_ref=dst,
                send_sem=self.send_sems.at[used],
                recv_sem=self.recv_sems.at[used],
                device_id=device,
                device_id_type=MESH,
            )

        describe().start()
        made = Copy(describe)
        self.started.append(made)
        return made

    def finish(self):
        for made in self.started:
            made.wait_send()


def rows_at(start, size):
    return pl.ds(pl.multiple_of(start, TILE), size)


class Around:
    def __init__(self, here):
        self.here = here
        self.other = here.at(dcore=1)
        self.across = here.at(dzl=1)
        self.ahead = [here.at(dx=step) for step in (1, 2, 3)]
        self.beside = [here.at(dy=step) for step in (1, 2, 3)]
        self.levels = [here.at(dzh=step) for step in (2, 1, 3)]

    def everyone(self):
        here = self.here
        group = [here.at(dx=dx, dzl=dzl) for dx in range(4) for dzl in range(2) if dx or dzl]
        return [self.other] + group + self.beside + self.levels


def gather_steps(around, send, gathered):
    here = around.here
    made = {}

    def move(start, size, device):
        def ends():
            block = gathered.at[pl.ds(start, size)]
            return block, block

        return send.copy(ends, device)

    def own():
        for dx, dzl in ((0, 1), (1, 0), (3, 0), (1, 1), (3, 1), (2, 0), (2, 1)):
            made[dx, dzl] = move(here.gather_tiles[0][0], 2, here.at(dx=dx, dzl=dzl))

    def to_core(dx):
        for dzl in range(2):
            if dx or dzl:
                made[-dx % 4, dzl].wait_recv()
        made[dx] = move(here.gather_pairs[dx], 4, around.other)

    def end():
        for dx in range(4):
            made[dx].wait_recv()

    steps = {"own": own, "end": end}
    for dx in range(4):
        steps[f"core{dx}"] = functools.partial(to_core, dx)
    return steps


def reduce_steps(
    around, send, parts, from_left, from_right, full_left, full_right, merged,
    level_send, level_recv, total, result,
):
    here = around.here
    right, left = around.beside[0], around.beside[2]
    by_right, by_left = (2, 1), (3, 0)
    level_of = {2: 0, 1: 1, 3: 2}
    firsts, lefts, rights, levels = {}, {}, {}, {}

    def where(dy, dzh):
        return rows_at(here.at(dy=dy, dzh=dzh)[1] * OWNED, OWNED)

    def first(number):
        dzh = by_right[number]
        firsts[dzh] = send.copy(
            lambda: (parts.at[where(2, by_right[number]), :], from_left.at[number]), right
        )
        dzh = by_left[number]
        firsts[dzh] = send.copy(
            lambda: (parts.at[where(2, by_left[number]), :], from_right.at[number]), left
        )

    def to_right(dzh, source):
        rights[dzh] = send.copy(lambda: (source(), full_left.at[dzh]), right)

    def to_left(dzh, source):
        lefts[dzh] = send.copy(lambda: (source(), full_right.at[dzh]), left)

    def plain():
        to_right(3, lambda: parts.at[where(1, 3), :])
        to_left(2, lambda: parts.at[where(-1, 2), :])

    def merge_right(number):
        dzh = by_right[number]
        firsts[dzh].wait_recv()
        merged[dzh] = (
            parts[where(1, dzh), :].astype(F32) + from_left[number].astype(F32)
        ).astype(BF16)
        to_right(dzh, lambda: merged.at[dzh])

    def merge_left(number):
        dzh = by_left[number]
        firsts[dzh].wait_recv()
        merged[dzh] = (
            parts[where(-1, dzh), :].astype(F32) + from_right[number].astype(F32)
        ).astype(BF16)
        to_left(dzh, lambda: merged.at[dzh])

    def merge():
        merge_right(0)
        merge_left(0)

    def late():
        to_left(1, lambda: parts.at[where(-1, 1), :])
        merge_right(1)

    def last():
        to_right(0, lambda: parts.at[where(1, 0), :])
        merge_left(1)

    def complete(dzh):
        rights[dzh].wait_recv()
        lefts[dzh].wait_recv()
        summed = (
            parts[where(0, dzh), :].astype(F32)
            + full_left[dzh].astype(F32)
            + full_right[dzh].astype(F32)
        )
        if dzh:
            slot = level_of[dzh]
            level_send[slot] = summed.astype(BF16)
            levels[slot] = send.copy(
                lambda: (level_send.at[slot], level_recv.at[slot]), around.levels[slot]
            )
        else:
            total[...] = summed

    def end():
        for slot in range(3):
            levels[slot].wait_recv()
        result[...] = (
            total[...]
            + level_recv[0].astype(F32)
            + level_recv[1].astype(F32)
            + level_recv[2].astype(F32)
        ).astype(BF16)

    steps = {"plain": plain, "merge": merge, "late": late, "last": last, "end": end}
    for number in range(2):
        steps[f"first{number}"] = functools.partial(first, number)
    for dzh in range(4):
        steps[f"sum{dzh}"] = functools.partial(complete, dzh)
    return steps


def spread_steps(around, send, gathered):
    here = around.here
    right, left = around.beside[0], around.beside[2]
    up, ring_right, ring_left, relays = {}, {}, {}, []
    came = {0: 2, 1: 3, 2: 1}

    def move(dy, dzh, device):
        def ends():
            block = gathered.at[pl.ds(here.at(dy=dy, dzh=dzh)[1] * 2, 2)]
            return block, block

        return send.copy(ends, device)

    def ring(dzh):
        ring_right[dzh] = move(0, dzh, right)
        ring_left[dzh] = move(0, dzh, left)

    def begin():
        up[1] = move(0, 0, around.levels[1])
        up[2] = move(0, 0, around.levels[2])
        ring(0)

    def far():
        up[0] = move(0, 0, around.levels[0])

    def level(slot):
        up[slot].wait_recv()
        ring(came[slot])
        if slot == 0:
            relays.append(move(0, 2, around.beside[1]))

    def relay(dzh):
        if dzh == 0:
            ring_right[dzh].wait_recv()
            relays.append(move(-1, dzh, right))
        else:
            ring_left[dzh].wait_recv()
            relays.append(move(1, dzh, left))

    def end():
        for dzh in (0, 2):
            ring_left[dzh].wait_recv()
        for dzh in (1, 2, 3):
            ring_right[dzh].wait_recv()
        for made in relays:
            made.wait_recv()

    steps = {"begin": begin, "far": far, "end": end}
    for slot in range(3):
        steps[f"level{slot}"] = functools.partial(level, slot)
    for dzh in (0, 1, 3):
        steps[f"relay{dzh}"] = functools.partial(relay, dzh)
    return steps


def scatter_steps(around, send, parts, out, core_recv, sent, received):
    here = around.here
    cores, made = [], {}

    def begin():
        for step in range(2):
            start = here.scatter_groups[1][1 - step] * TILE
            cores.append(
                send.copy(
                    lambda start=start, step=step: (
                        parts.at[rows_at(start, 4 * OWNED), :], core_recv.at[step]
                    ),
                    around.other,
                )
            )

    def collect(dx, step):
        spot = here.scatter_spots[dx]
        mine = rows_at((here.scatter_groups[0][1 - step] + spot) * TILE, OWNED)
        theirs = rows_at(spot * TILE, OWNED)
        return parts[mine, :].astype(F32) + core_recv[step, theirs, :].astype(F32)

    def chips(step):
        cores[step].wait_recv()
        for dx in (2, 1, 3, 0):
            slot = 4 * step + dx
            if slot != 4:
                sent[slot] = collect(dx, step).astype(BF16)
                made[slot] = send.copy(
                    lambda slot=slot: (sent.at[slot], received.at[slot]),
                    here.at(dx=dx, dzl=1 - step),
                )

    def end():
        summed = collect(0, 1)
        for slot in made:
            made[slot].wait_recv()
        for slot in made:
            summed = summed + received[slot].astype(F32)
        out[...] = summed.astype(BF16)

    return {
        "cores": begin,
        "chips0": functools.partial(chips, 0),
        "chips1": functools.partial(chips, 1),
        "end": end,
    }


def weight_steps(
    around, send, term, grad_weight, term_core, term_across, term_x, term_y, term_z, chunk_sum
):
    here = around.here
    half_mine = here.core * 128
    half_other = 128 - half_mine
    quarter_mine = half_mine + here.zl * 64
    quarter_other = half_mine + 64 - here.zl * 64
    piece_mine = quarter_mine + here.x * 16
    state = {}

    def lines(start, size):
        return pl.ds(pl.multiple_of(start, size), size)

    def same(start, size, device):
        def ends():
            block = grad_weight.at[lines(start, size), :]
            return block, block

        return send.copy(ends, device)

    def core():
        state["core"] = send.copy(lambda: (term.at[lines(half_other, 128), :], term_core), around.other)

    def across():
        state["core"].wait_recv()
        mine = lines(half_mine, 128)
        term[mine, :] = term[mine, :] + term_core[...]
        state["across"] = send.copy(lambda: (term.at[lines(quarter_other, 64), :], term_across), around.across)

    def along():
        state["across"].wait_recv()
        mine = lines(quarter_mine, 64)
        term[mine, :] = term[mine, :] + term_across[...]
        state["x"] = [
            send.copy(lambda dx=dx: (term.at[lines(quarter_mine + lax.rem(here.x + dx, jnp.int32(4)) * 16, 16), :], term_x.at[dx - 1]), around.ahead[dx - 1])
            for dx in (1, 2, 3)
        ]

    def over_y():
        for made in state["x"]:
            made.wait_recv()
        chunk_sum[0] = term[lines(piece_mine, 16), :] + term_x[0] + term_x[1] + term_x[2]
        state["y"] = [
            send.copy(lambda slot=slot: (chunk_sum.at[0], term_y.at[slot]), around.beside[slot]) for slot in range(3)
        ]

    def over_z():
        for made in state["y"]:
            made.wait_recv()
        chunk_sum[1] = (chunk_sum[0] + term_y[1]) + (term_y[0] + term_y[2])
        state["z"] = [
            send.copy(lambda slot=slot: (chunk_sum.at[1], term_z.at[slot]), around.levels[slot]) for slot in range(3)
        ]

    def whole_x():
        for made in state["z"]:
            made.wait_recv()
        piece = lines(piece_mine, 16)
        grad_weight[piece, :] = (chunk_sum[1] + term_z[0]) + (term_z[1] + term_z[2])
        state["all_x"] = [same(piece_mine, 16, around.ahead[slot]) for slot in range(3)]

    def whole_across():
        for made in state["all_x"]:
            made.wait_recv()
        state["all_across"] = same(quarter_mine, 64, around.across)

    def whole_core():
        state["all_across"].wait_recv()
        state["all_core"] = same(half_mine, 128, around.other)

    def end():
        state["all_core"].wait_recv()

    found = (core, across, along, over_y, over_z, whole_x, whole_across, whole_core, end)
    return {f"weight{number}": step for number, step in enumerate(found)}


def run(streams, names):
    for name in names:
        stream, step = name.split(".")
        streams[stream][step]()


def layer_kernel(
    count, tile_row, tile_col, features, weight, cotangent, tiles,
    output, grad_weight, grad_input, *rest
):
    (
        sources, backs, parts, parts_back, held, prefix, running,
        reduce_scratch, scatter_scratch, results, grads,
        term, term_core, term_across, term_x, term_y, term_z, chunk_sum,
        plan_lines, plan, plan_sem, tile_sem, send_sems, recv_sems,
    ) = rest
    slots = held.shape[0]
    share = slots // LOADS
    loads = [
        pltpu.make_async_copy(
            tiles.at[pl.ds(number * share, share)],
            held.at[pl.ds(number * share, share)],
            tile_sem.at[number],
        )
        for number in range(LOADS)
    ]
    for load in loads:
        load.start()
    around = Around(Place())
    here = around.here
    barrier = pltpu.get_barrier_semaphore()
    devices = around.everyone()
    for device in devices:
        pl.semaphore_signal(barrier, inc=1, device_id=device, device_id_type=MESH)
    pl.semaphore_wait(barrier, len(devices))
    send = Sender(send_sems, recv_sems)
    columns = [pl.ds(half * HALF, HALF) for half in range(2)]

    def product(line, transposed, half, source, placed, services):
        contract = 0 if transposed else 1
        running[...] = jnp.zeros_like(running)

        def group(number, carry):
            for at, names in services:
                @pl.when(number == at)
                def _():
                    run(streams, names)

            for step in range(GROUP):
                slot = number * GROUP + step
                block = source[plan[line + 1, slot]]
                fresh = lax.dot_general(
                    held[plan[line, slot]],
                    block,
                    (((contract,), (0,)), ((), ())),
                    preferred_element_type=F32,
                )
                running[...] = fresh + plan[line + 2, slot].astype(F32) * running[...]
                prefix[slot] = running[...].astype(BF16)
            return carry

        lax.fori_loop(0, slots // GROUP, group, 0)

        def place(tile, carry):
            placed[rows_at(tile * TILE, TILE), :] = prefix[plan[line + 3, tile]]
            return carry

        lax.fori_loop(0, TILES, place, 0, unroll=4)

    streams = {}
    mine = here.gather_tiles[0][0]
    for half in range(2):
        for part in range(2):
            sources[half][mine + part] = features[pl.ds(part * TILE, TILE), columns[half]]
        streams[f"g{half}"] = gather_steps(around, send, sources[half])
        streams[f"r{half}"] = reduce_steps(
            around, send, parts[half], *[ref.at[half] for ref in reduce_scratch], results.at[half]
        )
        streams[f"s{half}"] = spread_steps(around, send, backs[half])
        streams[f"c{half}"] = scatter_steps(
            around, send, parts_back[half], grads.at[half],
            *[ref.at[half] for ref in scatter_scratch],
        )
    streams["w"] = weight_steps(
        around, send, term, grad_weight, term_core, term_across, term_x, term_y, term_z, chunk_sum
    )
    run(streams, GATHER_BEGIN)
    prefix[slots] = jnp.zeros((TILE, HALF), BF16)
    live = count[0]
    rows = tile_row[...]
    cols = tile_col[...]
    found = arrange(rows, gather_place(cols), live) + arrange(scatter_place(cols), rows, live)
    for line, value in enumerate(found):
        plan_lines[line : line + 1, :] = value
    load_plan = pltpu.make_async_copy(plan_lines, plan, plan_sem)
    load_plan.start()
    run(streams, GATHER_FIRST)
    for load in loads:
        load.wait()
    load_plan.wait()
    product(0, False, 0, sources[0], parts[0], GATHER_DURING)
    run(streams, GATHER_LAST)
    run(streams, REDUCE_FIRST)
    product(0, False, 1, sources[1], parts[1], REDUCE_DURING)
    run(streams, REDUCE_LAST)

    gathered = jnp.concatenate([results[0], results[1]], axis=1)
    preact = jnp.dot(gathered, weight[...], preferred_element_type=F32)
    squared = preact * preact
    bent = jnp.tanh(SLOPE * (preact + 0.044715 * (preact * squared)))
    slope = 0.5 * (1.0 + bent) + 0.5 * preact * (1.0 - bent * bent) * (
        SLOPE * (1.0 + 3 * 0.044715 * squared)
    )
    delta = (cotangent[...].astype(F32) * slope).astype(BF16)
    back = lax.dot_general(
        delta, weight[...], (((1,), (1,)), ((), ())), preferred_element_type=F32
    ).astype(BF16)
    mine = here.at()[1] * 2
    for half in range(2):
        for part in range(2):
            backs[half][mine + part] = back[
                part * TILE : (part + 1) * TILE, half * HALF : (half + 1) * HALF
            ]
    run(streams, SPREAD_BEGIN)
    output[...] = (0.5 * preact * (1.0 + bent)).astype(BF16)
    term[...] = lax.dot_general(
        gathered, delta, (((0,), (0,)), ((), ())), preferred_element_type=F32
    )
    run(streams, SPREAD_FIRST)
    product(4, True, 0, backs[0], parts_back[0], SPREAD_DURING)
    run(streams, SPREAD_LAST)
    product(4, True, 1, backs[1], parts_back[1], SCATTER_DURING)
    run(streams, SCATTER_LAST)
    for half in range(2):
        grad_input[:, columns[half]] = grads[half]
    send.finish()


def layer(count, tile_row, tile_col, features, weight, cotangent, tiles):
    slots = tiles.shape[0]
    block = (TILE, HALF)
    full = (OWNED, HALF)
    nodes = pltpu.VMEM((NODES, HALF), BF16)
    stacked = pltpu.VMEM((TILES, TILE, HALF), BF16)

    single = pltpu.VMEM((2,) + full, BF16)

    def pair(lead):
        return pltpu.VMEM((2, lead) + full, BF16)

    return pl.pallas_call(
        layer_kernel,
        out_shape=(
            jax.ShapeDtypeStruct((OWNED, WIDTH), BF16),
            jax.ShapeDtypeStruct((WIDTH, WIDTH), F32),
            jax.ShapeDtypeStruct((OWNED, WIDTH), BF16),
        ),
        in_specs=[SMEM_SPEC] + [VMEM_SPEC] * 5 + [ANY_SPEC],
        out_specs=(VMEM_SPEC,) * 3,
        scratch_shapes=[
            [stacked, stacked],
            [stacked, stacked],
            [nodes, nodes],
            [nodes, nodes],
            pltpu.VMEM((slots, TILE, TILE), BF16),
            pltpu.VMEM((slots + 1,) + block, BF16),
            pltpu.VMEM(block, F32),
            [pair(lead) for lead in (2, 2, 4, 4, 4, 3, 3)] + [pltpu.VMEM((2,) + full, F32)],
            [pltpu.VMEM((2, 2, 4 * OWNED, HALF), BF16), pair(8), pair(8)],
            single,
            single,
            pltpu.VMEM((WIDTH, WIDTH), F32),
            pltpu.VMEM((128, WIDTH), F32),
            pltpu.VMEM((64, WIDTH), F32),
            pltpu.VMEM((3, 16, WIDTH), F32),
            pltpu.VMEM((3, 16, WIDTH), F32),
            pltpu.VMEM((3, 16, WIDTH), F32),
            pltpu.VMEM((2, 16, WIDTH), F32),
            pltpu.VMEM((8, slots), jnp.int32),
            pltpu.SMEM((8, slots), jnp.int32),
            pltpu.SemaphoreType.DMA,
            pltpu.SemaphoreType.DMA((LOADS,)),
            pltpu.SemaphoreType.DMA((COPIES,)),
            pltpu.SemaphoreType.DMA((COPIES,)),
        ],
        compiler_params=pltpu.CompilerParams(
            collective_id=0, has_side_effects=True, vmem_limit_bytes=VMEM_LIMIT
        ),
        name="layer",
    )(count, tile_row, tile_col, features, weight, cotangent, tiles)


def hand_on_kernel(*refs):
    for number in range(3):
        refs[number + 3][...] = refs[number][...]


def hand_on(*arrays):
    return pl.pallas_call(
        hand_on_kernel,
        out_shape=tuple(jax.ShapeDtypeStruct(array.shape, array.dtype) for array in arrays),
        in_specs=[VMEM_SPEC] * 3,
        out_specs=(VMEM_SPEC,) * 3,
        name="hand_on",
    )(*arrays)


def shards(features, weight, adjacency, tile_row, tile_col, tile_count, cotangent):
    return hand_on(
        *layer(
            tile_count[0], tile_row[0], tile_col[0], features, weight, cotangent, adjacency[0, 0]
        )
    )


def solution(mesh):
    return jax.shard_map(
        shards,
        mesh=mesh,
        in_specs=(
            P(("row", "col"), None),
            P(),
            P("row", "col", None, None, None),
            P("row", "col", None),
            P("row", "col", None),
            P("row", "col"),
            P(("row", "col"), None),
        ),
        out_specs=(P(("row", "col"), None), P(), P(("row", "col"), None)),
        check_vma=False,
    )
```

```python
import functools
import math

import jax
import jax.numpy as jnp
from jax import lax
from jax.experimental import pallas as pl
from jax.experimental.pallas import tpu as pltpu
from jax.sharding import PartitionSpec as P

MESH = pl.DeviceIdType.MESH
BF16 = jnp.bfloat16
F32 = jnp.float32
TILE = 128
OWNED = 256
WIDTH = 256
HALF = 128
NODES = 4096
TILES = NODES // TILE
GROUP = 64
COPIES = 128
BY_RIGHT = ((0,), (0, 3))
LOADS = 4
GATHER_BEGIN = ("g0.own", "g1.own",)
GATHER_FIRST = ("g0.core0", "g0.core1", "g0.core3", "g0.core2", "g0.end",)
GATHER_DURING = ((1,("g1.core0","g1.core1","g1.core3","g1.core2")),)
GATHER_LAST = ("g1.end",)
REDUCE_FIRST = ("r0.first0", "r0.first1", "r0.plain",)
REDUCE_DURING = ((2,("r0.merge",)),)
REDUCE_LAST = ("r0.late", "r0.last", "r1.first0", "r1.first1", "r1.plain", "r0.sum2", "r0.sum3", "r0.sum1", "r0.sum0", "r1.merge", "r1.late", "r1.last", "r0.end", "r1.sum2", "r1.sum3", "r1.sum1", "r1.sum0", "r1.end",)
SPREAD_BEGIN = ("s0.begin", "s0.far", "s1.begin", "s1.far",)
SPREAD_FIRST = ("w.weight0", "s0.relay0", "s1.relay0", "s0.level1", "s0.level2", "s0.level0", "s0.relay3", "s0.relay1", "w.weight1", "s1.level1", "s1.level2", "s1.level0", "w.weight2", "s0.end",)
SPREAD_DURING = ((1,("s1.relay3",)),(2,("s1.relay1","w.weight3")))
SPREAD_LAST = ("c0.cores", "s1.end", "w.weight4",)
SCATTER_DURING = ((1,("c0.chips0","c0.chips1","w.weight5")),(2,("w.weight6",)))
SCATTER_LAST = ("c1.cores", "w.weight7", "c1.chips0", "c1.chips1", "w.weight8", "c0.end", "c1.end",)
VMEM_LIMIT = 58 * 1024 * 1024
SLOPE = math.sqrt(2 / math.pi)

VMEM_SPEC = pl.BlockSpec(memory_space=pltpu.VMEM)
SMEM_SPEC = pl.BlockSpec(memory_space=pltpu.SMEM)
ANY_SPEC = pl.BlockSpec(memory_space=pl.ANY)
LOW = pl.ds(0, TILE)
HIGH = pl.ds(TILE, TILE)


def gather_place(tile):
    return (tile & 2) * 8 + (tile >> 3) * 4 + ((tile >> 2) & 1) * 2 + (tile & 1)


def scatter_place(tile):
    return (tile & 2) * 8 + ((tile >> 2) & 1) * 8 + (tile >> 3) * 2 + (tile & 1)


def arrange(placed, taken, live):
    slots = placed.shape[1]
    lane = lax.broadcasted_iota(jnp.int32, (slots, slots), 1)
    line = lax.broadcasted_iota(jnp.int32, (slots, slots), 0)

    def turned(flat):
        return jnp.sum(jnp.where(lane == line, flat, 0), axis=1, keepdims=True)

    lane_row = lax.broadcasted_iota(jnp.int32, (1, slots), 1)
    tagged = jnp.where(lane_row < live, placed, TILES)
    key = tagged * 256 + lane_row
    rank = jnp.sum(jnp.where(key < turned(key), 1, 0), axis=1, keepdims=True)
    tag_line = turned(tagged)
    taken_line = turned(taken)
    chosen = rank == lane

    def pick(column):
        return jnp.sum(jnp.where(chosen, column, 0), axis=0, keepdims=True)

    order = pick(line)
    source = pick(taken_line)
    tag = pick(tag_line + 1)
    before = jnp.sum(jnp.where(rank + 1 == lane, tag_line + 1, 0), axis=0, keepdims=True)
    keep = jnp.where(tag == before, 1, 0)
    up_to = jnp.sum(jnp.where(tag_line <= lane, 1, 0), axis=0, keepdims=True)
    here = jnp.sum(jnp.where(tag_line == lane, 1, 0), axis=0, keepdims=True)
    last = jnp.where(here > 0, up_to - 1, slots)
    return (order, source, keep, last)


class Place:
    def __init__(self):
        row = lax.axis_index("row")
        col = lax.axis_index("col")
        four, two = jnp.int32(4), jnp.int32(2)
        self.x = lax.div(row, four)
        self.zl = lax.rem(lax.div(row, two), two)
        self.core = lax.rem(row, two)
        self.y = lax.div(col, four)
        self.zh = lax.rem(col, four)
        xs = [lax.rem(self.x + step, four) * 4 for step in range(4)]
        zls = [self.zl * 2, 2 - self.zl * 2]
        cores = [self.core, 1 - self.core]
        ys = [lax.rem(self.y + step, four) * 4 for step in range(4)]
        zhs = [lax.rem(self.zh + step, four) for step in range(4)]
        self.rows = [[[x + zl + core for core in cores] for zl in zls] for x in xs]
        self.gather_tiles = [[cores[0] * 16 + x + zl for zl in zls] for x in xs]
        self.gather_pairs = [cores[0] * 16 + x for x in xs]
        self.scatter_groups = [[core * 16 + zl * 4 for zl in zls] for core in cores]
        self.scatter_spots = [lax.rem(self.x + step, four) * 2 for step in range(4)]
        self.cols = [[y + zh for zh in zhs] for y in ys]

    def at(self, dx=0, dzl=0, dcore=0, dy=0, dzh=0):
        return (self.rows[dx % 4][dzl % 2][dcore % 2], self.cols[dy % 4][dzh % 4])


class Copy:
    def __init__(self, describe):
        self.describe = describe

    def wait_recv(self):
        self.describe().wait_recv()

    def wait_send(self):
        self.describe().wait_send()


class Sender:
    def __init__(self, send_sems, recv_sems):
        self.send_sems = send_sems
        self.recv_sems = recv_sems
        self.started = []

    def copy(self, ends, device):
        used = len(self.started)

        def describe():
            src, dst = ends()
            return pltpu.make_async_remote_copy(
                src_ref=src,
                dst_ref=dst,
                send_sem=self.send_sems.at[used],
                recv_sem=self.recv_sems.at[used],
                device_id=device,
                device_id_type=MESH,
            )

        describe().start()
        made = Copy(describe)
        self.started.append(made)
        return made

    def finish(self):
        for made in self.started:
            made.wait_send()


def rows_at(start, size):
    return pl.ds(pl.multiple_of(start, TILE), size)


class Around:
    def __init__(self, here):
        self.here = here
        self.other = here.at(dcore=1)
        self.across = here.at(dzl=1)
        self.ahead = [here.at(dx=step) for step in (1, 2, 3)]
        self.beside = [here.at(dy=step) for step in (1, 2, 3)]
        self.levels = [here.at(dzh=step) for step in (2, 1, 3)]

    def everyone(self):
        here = self.here
        group = [here.at(dx=dx, dzl=dzl) for dx in range(4) for dzl in range(2) if dx or dzl]
        return [self.other] + group + self.beside + self.levels


def gather_steps(around, send, gathered):
    here = around.here
    made = {}

    def move(start, size, device):
        def ends():
            block = gathered.at[pl.ds(start, size)]
            return block, block

        return send.copy(ends, device)

    def own():
        for dx, dzl in ((0, 1), (1, 0), (3, 0), (1, 1), (3, 1), (2, 0), (2, 1)):
            made[dx, dzl] = move(here.gather_tiles[0][0], 2, here.at(dx=dx, dzl=dzl))

    def to_core(dx):
        for dzl in range(2):
            if dx or dzl:
                made[-dx % 4, dzl].wait_recv()
        made[dx] = move(here.gather_pairs[dx], 4, around.other)

    def end():
        for dx in range(4):
            made[dx].wait_recv()

    steps = {"own": own, "end": end}
    for dx in range(4):
        steps[f"core{dx}"] = functools.partial(to_core, dx)
    return steps


def reduce_steps(
    around, send, parts, from_left, from_right, full_left, full_right, merged,
    level_send, level_recv, total, result,
):
    here = around.here
    right, left = around.beside[0], around.beside[2]
    by_right, by_left = (2, 1), (3, 0)
    level_of = {2: 0, 1: 1, 3: 2}
    firsts, lefts, rights, levels = {}, {}, {}, {}

    def where(dy, dzh):
        return rows_at(here.at(dy=dy, dzh=dzh)[1] * OWNED, OWNED)

    def first(number):
        dzh = by_right[number]
        firsts[dzh] = send.copy(
            lambda: (parts.at[where(2, by_right[number]), :], from_left.at[number]), right
        )
        dzh = by_left[number]
        firsts[dzh] = send.copy(
            lambda: (parts.at[where(2, by_left[number]), :], from_right.at[number]), left
        )

    def to_right(dzh, source):
        rights[dzh] = send.copy(lambda: (source(), full_left.at[dzh]), right)

    def to_left(dzh, source):
        lefts[dzh] = send.copy(lambda: (source(), full_right.at[dzh]), left)

    def plain():
        to_right(3, lambda: parts.at[where(1, 3), :])
        to_left(2, lambda: parts.at[where(-1, 2), :])

    def merge_right(number):
        dzh = by_right[number]
        firsts[dzh].wait_recv()
        merged[dzh] = (
            parts[where(1, dzh), :].astype(F32) + from_left[number].astype(F32)
        ).astype(BF16)
        to_right(dzh, lambda: merged.at[dzh])

    def merge_left(number):
        dzh = by_left[number]
        firsts[dzh].wait_recv()
        merged[dzh] = (
            parts[where(-1, dzh), :].astype(F32) + from_right[number].astype(F32)
        ).astype(BF16)
        to_left(dzh, lambda: merged.at[dzh])

    def merge():
        merge_right(0)
        merge_left(0)

    def late():
        to_left(1, lambda: parts.at[where(-1, 1), :])
        merge_right(1)

    def last():
        to_right(0, lambda: parts.at[where(1, 0), :])
        merge_left(1)

    def complete(dzh):
        rights[dzh].wait_recv()
        lefts[dzh].wait_recv()
        summed = (
            parts[where(0, dzh), :].astype(F32)
            + full_left[dzh].astype(F32)
            + full_right[dzh].astype(F32)
        )
        if dzh:
            slot = level_of[dzh]
            level_send[slot] = summed.astype(BF16)
            levels[slot] = send.copy(
                lambda: (level_send.at[slot], level_recv.at[slot]), around.levels[slot]
            )
        else:
            total[...] = summed

    def end():
        for slot in range(3):
            levels[slot].wait_recv()
        result[...] = (
            total[...]
            + level_recv[0].astype(F32)
            + level_recv[1].astype(F32)
            + level_recv[2].astype(F32)
        ).astype(BF16)

    steps = {"plain": plain, "merge": merge, "late": late, "last": last, "end": end}
    for number in range(2):
        steps[f"first{number}"] = functools.partial(first, number)
    for dzh in range(4):
        steps[f"sum{dzh}"] = functools.partial(complete, dzh)
    return steps


def spread_steps(around, send, gathered, by_right):
    here = around.here
    right, left = around.beside[0], around.beside[2]
    up, ring_right, ring_left, relays = {}, {}, {}, []
    came = {0: 2, 1: 3, 2: 1}

    def move(dy, dzh, device):
        def ends():
            block = gathered.at[pl.ds(here.at(dy=dy, dzh=dzh)[1] * 2, 2)]
            return block, block

        return send.copy(ends, device)

    def ring(dzh):
        ring_right[dzh] = move(0, dzh, right)
        ring_left[dzh] = move(0, dzh, left)

    def begin():
        up[1] = move(0, 0, around.levels[1])
        up[2] = move(0, 0, around.levels[2])
        ring(0)

    def far():
        up[0] = move(0, 0, around.levels[0])

    def level(slot):
        up[slot].wait_recv()
        ring(came[slot])
        if slot == 0:
            relays.append(move(0, 2, around.beside[1]))

    def relay(dzh):
        if dzh in by_right:
            ring_right[dzh].wait_recv()
            relays.append(move(-1, dzh, right))
        else:
            ring_left[dzh].wait_recv()
            relays.append(move(1, dzh, left))

    def end():
        for dzh in range(4):
            if dzh == 2 or dzh in by_right:
                ring_left[dzh].wait_recv()
            if dzh not in by_right:
                ring_right[dzh].wait_recv()
        for made in relays:
            made.wait_recv()

    steps = {"begin": begin, "far": far, "end": end}
    for slot in range(3):
        steps[f"level{slot}"] = functools.partial(level, slot)
    for dzh in (0, 1, 3):
        steps[f"relay{dzh}"] = functools.partial(relay, dzh)
    return steps


def scatter_steps(around, send, parts, out, core_recv, sent, received):
    here = around.here
    cores, made = [], {}

    def begin():
        for step in range(2):
            start = here.scatter_groups[1][1 - step] * TILE
            cores.append(
                send.copy(
                    lambda start=start, step=step: (
                        parts.at[rows_at(start, 4 * OWNED), :], core_recv.at[step]
                    ),
                    around.other,
                )
            )

    def collect(dx, step):
        spot = here.scatter_spots[dx]
        mine = rows_at((here.scatter_groups[0][1 - step] + spot) * TILE, OWNED)
        theirs = rows_at(spot * TILE, OWNED)
        return parts[mine, :].astype(F32) + core_recv[step, theirs, :].astype(F32)

    def chips(step):
        cores[step].wait_recv()
        for dx in (2, 1, 3, 0):
            slot = 4 * step + dx
            if slot != 4:
                sent[slot] = collect(dx, step).astype(BF16)
                made[slot] = send.copy(
                    lambda slot=slot: (sent.at[slot], received.at[slot]),
                    here.at(dx=dx, dzl=1 - step),
                )

    def end():
        summed = collect(0, 1)
        for slot in made:
            made[slot].wait_recv()
        for slot in made:
            summed = summed + received[slot].astype(F32)
        out[...] = summed.astype(BF16)

    return {
        "cores": begin,
        "chips0": functools.partial(chips, 0),
        "chips1": functools.partial(chips, 1),
        "end": end,
    }


def weight_steps(
    around, send, term, grad_weight, term_core, term_across, term_x, term_y, term_z, chunk_sum
):
    here = around.here
    half_mine = here.core * 128
    half_other = 128 - half_mine
    quarter_mine = half_mine + here.zl * 64
    quarter_other = half_mine + 64 - here.zl * 64
    piece_mine = quarter_mine + here.x * 16
    state = {}

    def lines(start, size):
        return pl.ds(pl.multiple_of(start, size), size)

    def same(start, size, device):
        def ends():
            block = grad_weight.at[lines(start, size), :]
            return block, block

        return send.copy(ends, device)

    def core():
        state["core"] = send.copy(lambda: (term.at[lines(half_other, 128), :], term_core), around.other)

    def across():
        state["core"].wait_recv()
        mine = lines(half_mine, 128)
        term[mine, :] = term[mine, :] + term_core[...]
        state["across"] = send.copy(lambda: (term.at[lines(quarter_other, 64), :], term_across), around.across)

    def along():
        state["across"].wait_recv()
        mine = lines(quarter_mine, 64)
        term[mine, :] = term[mine, :] + term_across[...]
        state["x"] = [
            send.copy(lambda dx=dx: (term.at[lines(quarter_mine + lax.rem(here.x + dx, jnp.int32(4)) * 16, 16), :], term_x.at[dx - 1]), around.ahead[dx - 1])
            for dx in (1, 2, 3)
        ]

    def over_y():
        for made in state["x"]:
            made.wait_recv()
        chunk_sum[0] = term[lines(piece_mine, 16), :] + term_x[0] + term_x[1] + term_x[2]
        state["y"] = [
            send.copy(lambda slot=slot: (chunk_sum.at[0], term_y.at[slot]), around.beside[slot]) for slot in range(3)
        ]

    def over_z():
        for made in state["y"]:
            made.wait_recv()
        chunk_sum[1] = (chunk_sum[0] + term_y[1]) + (term_y[0] + term_y[2])
        state["z"] = [
            send.copy(lambda slot=slot: (chunk_sum.at[1], term_z.at[slot]), around.levels[slot]) for slot in range(3)
        ]

    def whole_x():
        for made in state["z"]:
            made.wait_recv()
        piece = lines(piece_mine, 16)
        grad_weight[piece, :] = (chunk_sum[1] + term_z[0]) + (term_z[1] + term_z[2])
        state["all_x"] = [same(piece_mine, 16, around.ahead[slot]) for slot in range(3)]

    def whole_across():
        for made in state["all_x"]:
            made.wait_recv()
        state["all_across"] = same(quarter_mine, 64, around.across)

    def whole_core():
        state["all_across"].wait_recv()
        state["all_core"] = same(half_mine, 128, around.other)

    def end():
        state["all_core"].wait_recv()

    found = (core, across, along, over_y, over_z, whole_x, whole_across, whole_core, end)
    return {f"weight{number}": step for number, step in enumerate(found)}


def run(streams, names):
    for name in names:
        stream, step = name.split(".")
        streams[stream][step]()


def layer_kernel(
    count, tile_row, tile_col, features, weight, cotangent, tiles,
    output, grad_weight, grad_input, *rest
):
    (
        sources, backs, parts, parts_back, held, prefix, running,
        reduce_scratch, scatter_scratch, results, grads,
        term, term_core, term_across, term_x, term_y, term_z, chunk_sum,
        plan_lines, plan, plan_sem, tile_sem, send_sems, recv_sems,
    ) = rest
    slots = held.shape[0]
    share = slots // LOADS
    loads = [
        pltpu.make_async_copy(
            tiles.at[pl.ds(number * share, share)],
            held.at[pl.ds(number * share, share)],
            tile_sem.at[number],
        )
        for number in range(LOADS)
    ]
    for load in loads:
        load.start()
    around = Around(Place())
    here = around.here
    barrier = pltpu.get_barrier_semaphore()
    devices = around.everyone()
    for device in devices:
        pl.semaphore_signal(barrier, inc=1, device_id=device, device_id_type=MESH)
    pl.semaphore_wait(barrier, len(devices))
    send = Sender(send_sems, recv_sems)
    columns = [pl.ds(half * HALF, HALF) for half in range(2)]

    def product(line, transposed, half, source, placed, services):
        contract = 0 if transposed else 1
        running[...] = jnp.zeros_like(running)

        def group(number, carry):
            for at, names in services:
                @pl.when(number == at)
                def _():
                    run(streams, names)

            for step in range(GROUP):
                slot = number * GROUP + step
                block = source[plan[line + 1, slot]]
                fresh = lax.dot_general(
                    held[plan[line, slot]],
                    block,
                    (((contract,), (0,)), ((), ())),
                    preferred_element_type=F32,
                )
                running[...] = fresh + plan[line + 2, slot].astype(F32) * running[...]
                prefix[slot] = running[...].astype(BF16)
            return carry

        lax.fori_loop(0, slots // GROUP, group, 0)

        def place(tile, carry):
            placed[rows_at(tile * TILE, TILE), :] = prefix[plan[line + 3, tile]]
            return carry

        lax.fori_loop(0, TILES, place, 0, unroll=4)

    streams = {}
    mine = here.gather_tiles[0][0]
    for half in range(2):
        for part in range(2):
            sources[half][mine + part] = features[pl.ds(part * TILE, TILE), columns[half]]
        streams[f"g{half}"] = gather_steps(around, send, sources[half])
        streams[f"r{half}"] = reduce_steps(
            around, send, parts[half], *[ref.at[half] for ref in reduce_scratch], results.at[half]
        )
        streams[f"s{half}"] = spread_steps(around, send, backs[half], BY_RIGHT[half])
        streams[f"c{half}"] = scatter_steps(
            around, send, parts_back[half], grads.at[half],
            *[ref.at[half] for ref in scatter_scratch],
        )
    streams["w"] = weight_steps(
        around, send, term, grad_weight, term_core, term_across, term_x, term_y, term_z, chunk_sum
    )
    run(streams, GATHER_BEGIN)
    prefix[slots] = jnp.zeros((TILE, HALF), BF16)
    live = count[0]
    rows = tile_row[...]
    cols = tile_col[...]
    found = arrange(rows, gather_place(cols), live) + arrange(scatter_place(cols), rows, live)
    for line, value in enumerate(found):
        plan_lines[line : line + 1, :] = value
    load_plan = pltpu.make_async_copy(plan_lines, plan, plan_sem)
    load_plan.start()
    run(streams, GATHER_FIRST)
    for load in loads:
        load.wait()
    load_plan.wait()
    product(0, False, 0, sources[0], parts[0], GATHER_DURING)
    run(streams, GATHER_LAST)
    run(streams, REDUCE_FIRST)
    product(0, False, 1, sources[1], parts[1], REDUCE_DURING)
    run(streams, REDUCE_LAST)

    gathered = jnp.concatenate([results[0], results[1]], axis=1)
    preact = jnp.dot(gathered, weight[...], preferred_element_type=F32)
    squared = preact * preact
    bent = jnp.tanh(SLOPE * (preact + 0.044715 * (preact * squared)))
    slope = 0.5 * (1.0 + bent) + 0.5 * preact * (1.0 - bent * bent) * (
        SLOPE * (1.0 + 3 * 0.044715 * squared)
    )
    delta = (cotangent[...].astype(F32) * slope).astype(BF16)
    back = lax.dot_general(
        delta, weight[...], (((1,), (1,)), ((), ())), preferred_element_type=F32
    ).astype(BF16)
    mine = here.at()[1] * 2
    for half in range(2):
        for part in range(2):
            backs[half][mine + part] = back[
                part * TILE : (part + 1) * TILE, half * HALF : (half + 1) * HALF
            ]
    run(streams, SPREAD_BEGIN)
    output[...] = (0.5 * preact * (1.0 + bent)).astype(BF16)
    term[...] = lax.dot_general(
        gathered, delta, (((0,), (0,)), ((), ())), preferred_element_type=F32
    )
    run(streams, SPREAD_FIRST)
    product(4, True, 0, backs[0], parts_back[0], SPREAD_DURING)
    run(streams, SPREAD_LAST)
    product(4, True, 1, backs[1], parts_back[1], SCATTER_DURING)
    run(streams, SCATTER_LAST)
    for half in range(2):
        grad_input[:, columns[half]] = grads[half]
    send.finish()


def layer(count, tile_row, tile_col, features, weight, cotangent, tiles):
    slots = tiles.shape[0]
    block = (TILE, HALF)
    full = (OWNED, HALF)
    nodes = pltpu.VMEM((NODES, HALF), BF16)
    stacked = pltpu.VMEM((TILES, TILE, HALF), BF16)

    single = pltpu.VMEM((2,) + full, BF16)

    def pair(lead):
        return pltpu.VMEM((2, lead) + full, BF16)

    return pl.pallas_call(
        layer_kernel,
        out_shape=(
            jax.ShapeDtypeStruct((OWNED, WIDTH), BF16),
            jax.ShapeDtypeStruct((WIDTH, WIDTH), F32),
            jax.ShapeDtypeStruct((OWNED, WIDTH), BF16),
        ),
        in_specs=[SMEM_SPEC] + [VMEM_SPEC] * 5 + [ANY_SPEC],
        out_specs=(VMEM_SPEC,) * 3,
        scratch_shapes=[
            [stacked, stacked],
            [stacked, stacked],
            [nodes, nodes],
            [nodes, nodes],
            pltpu.VMEM((slots, TILE, TILE), BF16),
            pltpu.VMEM((slots + 1,) + block, BF16),
            pltpu.VMEM(block, F32),
            [pair(lead) for lead in (2, 2, 4, 4, 4, 3, 3)] + [pltpu.VMEM((2,) + full, F32)],
            [pltpu.VMEM((2, 2, 4 * OWNED, HALF), BF16), pair(8), pair(8)],
            single,
            single,
            pltpu.VMEM((WIDTH, WIDTH), F32),
            pltpu.VMEM((128, WIDTH), F32),
            pltpu.VMEM((64, WIDTH), F32),
            pltpu.VMEM((3, 16, WIDTH), F32),
            pltpu.VMEM((3, 16, WIDTH), F32),
            pltpu.VMEM((3, 16, WIDTH), F32),
            pltpu.VMEM((2, 16, WIDTH), F32),
            pltpu.VMEM((8, slots), jnp.int32),
            pltpu.SMEM((8, slots), jnp.int32),
            pltpu.SemaphoreType.DMA,
            pltpu.SemaphoreType.DMA((LOADS,)),
            pltpu.SemaphoreType.DMA((COPIES,)),
            pltpu.SemaphoreType.DMA((COPIES,)),
        ],
        compiler_params=pltpu.CompilerParams(
            collective_id=0, has_side_effects=True, vmem_limit_bytes=VMEM_LIMIT
        ),
        name="layer",
    )(count, tile_row, tile_col, features, weight, cotangent, tiles)


def hand_on_kernel(*refs):
    for number in range(3):
        refs[number + 3][...] = refs[number][...]


def hand_on(*arrays):
    return pl.pallas_call(
        hand_on_kernel,
        out_shape=tuple(jax.ShapeDtypeStruct(array.shape, array.dtype) for array in arrays),
        in_specs=[VMEM_SPEC] * 3,
        out_specs=(VMEM_SPEC,) * 3,
        name="hand_on",
    )(*arrays)


def shards(features, weight, adjacency, tile_row, tile_col, tile_count, cotangent):
    return hand_on(
        *layer(
            tile_count[0], tile_row[0], tile_col[0], features, weight, cotangent, adjacency[0, 0]
        )
    )


def solution(mesh):
    return jax.shard_map(
        shards,
        mesh=mesh,
        in_specs=(
            P(("row", "col"), None),
            P(),
            P("row", "col", None, None, None),
            P("row", "col", None),
            P("row", "col", None),
            P("row", "col"),
            P(("row", "col"), None),
        ),
        out_specs=(P(("row", "col"), None), P(), P(("row", "col"), None)),
        check_vma=False,
    )
```

```python
import functools
import math

import jax
import jax.numpy as jnp
from jax import lax
from jax.experimental import pallas as pl
from jax.experimental.pallas import tpu as pltpu
from jax.sharding import PartitionSpec as P

MESH = pl.DeviceIdType.MESH
BF16 = jnp.bfloat16
F32 = jnp.float32
TILE = 128
OWNED = 256
WIDTH = 256
HALF = 128
NODES = 4096
TILES = NODES // TILE
GROUP = 64
COPIES = 128
BY_RIGHT = ((0,), (0, 3))
LOADS = 4
GATHER_BEGIN = ("g0.own", "g1.own",)
GATHER_FIRST = ("g0.core0", "g0.core1", "g0.core3", "g0.core2", "g0.end",)
GATHER_DURING = ((1,("g1.core0","g1.core1","g1.core3","g1.core2")),)
GATHER_LAST = ("g1.end",)
REDUCE_FIRST = ("r0.first0", "r0.first1", "r0.plain",)
REDUCE_DURING = ((2,("r0.merge",)),)
REDUCE_LAST = ("r0.late", "r0.last", "r1.first0", "r1.first1", "r1.plain", "r0.sum2", "r0.sum3", "r0.sum1", "r0.sum0", "r1.merge", "r1.late", "r1.last", "r0.end", "r1.sum2", "r1.sum3", "r1.sum1", "r1.sum0", "r1.end",)
SPREAD_BEGIN = ("s0.begin", "s1.begin")
SPREAD_FIRST = ("w.weight0", "s0.relay0", "s1.relay0", "s0.level1", "s0.level2", "s1.level1", "s1.level2", "s0.level0", "s0.relay3", "s0.relay1", "s1.level0", "w.weight1", "w.weight2", "s0.end")
SPREAD_DURING = ((1,("s1.relay3",)),(2,("s1.relay1","w.weight3")))
SPREAD_LAST = ("c0.cores", "s1.end", "w.weight4",)
SCATTER_DURING = ((1,("c0.chips0","c0.chips1","w.weight5")),(2,("w.weight6",)))
SCATTER_LAST = ("c1.cores", "w.weight7", "c1.chips0", "c1.chips1", "w.weight8", "c0.end", "c1.end",)
VMEM_LIMIT = 58 * 1024 * 1024
SLOPE = math.sqrt(2 / math.pi)

VMEM_SPEC = pl.BlockSpec(memory_space=pltpu.VMEM)
SMEM_SPEC = pl.BlockSpec(memory_space=pltpu.SMEM)
ANY_SPEC = pl.BlockSpec(memory_space=pl.ANY)
LOW = pl.ds(0, TILE)
HIGH = pl.ds(TILE, TILE)


def gather_place(tile):
    return (tile & 2) * 8 + (tile >> 3) * 4 + ((tile >> 2) & 1) * 2 + (tile & 1)


def scatter_place(tile):
    return (tile & 2) * 8 + ((tile >> 2) & 1) * 8 + (tile >> 3) * 2 + (tile & 1)


def arrange(placed, taken, live):
    slots = placed.shape[1]
    lane = lax.broadcasted_iota(jnp.int32, (slots, slots), 1)
    line = lax.broadcasted_iota(jnp.int32, (slots, slots), 0)

    def turned(flat):
        return jnp.sum(jnp.where(lane == line, flat, 0), axis=1, keepdims=True)

    lane_row = lax.broadcasted_iota(jnp.int32, (1, slots), 1)
    tagged = jnp.where(lane_row < live, placed, TILES)
    key = tagged * 256 + lane_row
    rank = jnp.sum(jnp.where(key < turned(key), 1, 0), axis=1, keepdims=True)
    tag_line = turned(tagged)
    taken_line = turned(taken)
    chosen = rank == lane

    def pick(column):
        return jnp.sum(jnp.where(chosen, column, 0), axis=0, keepdims=True)

    order = pick(line)
    source = pick(taken_line)
    tag = pick(tag_line + 1)
    before = jnp.sum(jnp.where(rank + 1 == lane, tag_line + 1, 0), axis=0, keepdims=True)
    keep = jnp.where(tag == before, 1, 0)
    up_to = jnp.sum(jnp.where(tag_line <= lane, 1, 0), axis=0, keepdims=True)
    here = jnp.sum(jnp.where(tag_line == lane, 1, 0), axis=0, keepdims=True)
    last = jnp.where(here > 0, up_to - 1, slots)
    return (order, source, keep, last)


class Place:
    def __init__(self):
        row = lax.axis_index("row")
        col = lax.axis_index("col")
        four, two = jnp.int32(4), jnp.int32(2)
        self.x = lax.div(row, four)
        self.zl = lax.rem(lax.div(row, two), two)
        self.core = lax.rem(row, two)
        self.y = lax.div(col, four)
        self.zh = lax.rem(col, four)
        xs = [lax.rem(self.x + step, four) * 4 for step in range(4)]
        zls = [self.zl * 2, 2 - self.zl * 2]
        cores = [self.core, 1 - self.core]
        ys = [lax.rem(self.y + step, four) * 4 for step in range(4)]
        zhs = [lax.rem(self.zh + step, four) for step in range(4)]
        self.rows = [[[x + zl + core for core in cores] for zl in zls] for x in xs]
        self.gather_tiles = [[cores[0] * 16 + x + zl for zl in zls] for x in xs]
        self.gather_pairs = [cores[0] * 16 + x for x in xs]
        self.scatter_groups = [[core * 16 + zl * 4 for zl in zls] for core in cores]
        self.scatter_spots = [lax.rem(self.x + step, four) * 2 for step in range(4)]
        self.cols = [[y + zh for zh in zhs] for y in ys]

    def at(self, dx=0, dzl=0, dcore=0, dy=0, dzh=0):
        return (self.rows[dx % 4][dzl % 2][dcore % 2], self.cols[dy % 4][dzh % 4])


class Copy:
    def __init__(self, describe):
        self.describe = describe

    def wait_recv(self):
        self.describe().wait_recv()

    def wait_send(self):
        self.describe().wait_send()


class Sender:
    def __init__(self, send_sems, recv_sems):
        self.send_sems = send_sems
        self.recv_sems = recv_sems
        self.started = []

    def copy(self, ends, device):
        used = len(self.started)

        def describe():
            src, dst = ends()
            return pltpu.make_async_remote_copy(
                src_ref=src,
                dst_ref=dst,
                send_sem=self.send_sems.at[used],
                recv_sem=self.recv_sems.at[used],
                device_id=device,
                device_id_type=MESH,
            )

        describe().start()
        made = Copy(describe)
        self.started.append(made)
        return made

    def finish(self):
        for made in self.started:
            made.wait_send()


def rows_at(start, size):
    return pl.ds(pl.multiple_of(start, TILE), size)


class Around:
    def __init__(self, here):
        self.here = here
        self.other = here.at(dcore=1)
        self.across = here.at(dzl=1)
        self.ahead = [here.at(dx=step) for step in (1, 2, 3)]
        self.beside = [here.at(dy=step) for step in (1, 2, 3)]
        self.levels = [here.at(dzh=step) for step in (2, 1, 3)]

    def everyone(self):
        here = self.here
        group = [here.at(dx=dx, dzl=dzl) for dx in range(4) for dzl in range(2) if dx or dzl]
        return [self.other] + group + self.beside + self.levels


def gather_steps(around, send, gathered):
    here = around.here
    made = {}

    def move(start, size, device):
        def ends():
            block = gathered.at[pl.ds(start, size)]
            return block, block

        return send.copy(ends, device)

    def own():
        for dx, dzl in ((0, 1), (1, 0), (3, 0), (1, 1), (3, 1), (2, 0), (2, 1)):
            made[dx, dzl] = move(here.gather_tiles[0][0], 2, here.at(dx=dx, dzl=dzl))

    def to_core(dx):
        for dzl in range(2):
            if dx or dzl:
                made[-dx % 4, dzl].wait_recv()
        made[dx] = move(here.gather_pairs[dx], 4, around.other)

    def end():
        for dx in range(4):
            made[dx].wait_recv()

    steps = {"own": own, "end": end}
    for dx in range(4):
        steps[f"core{dx}"] = functools.partial(to_core, dx)
    return steps


def reduce_steps(
    around, send, parts, from_left, from_right, full_left, full_right, merged,
    level_send, level_recv, total, result,
):
    here = around.here
    right, left = around.beside[0], around.beside[2]
    by_right, by_left = (2, 1), (3, 0)
    level_of = {2: 0, 1: 1, 3: 2}
    firsts, lefts, rights, levels = {}, {}, {}, {}

    def where(dy, dzh):
        return rows_at(here.at(dy=dy, dzh=dzh)[1] * OWNED, OWNED)

    def first(number):
        dzh = by_right[number]
        firsts[dzh] = send.copy(
            lambda: (parts.at[where(2, by_right[number]), :], from_left.at[number]), right
        )
        dzh = by_left[number]
        firsts[dzh] = send.copy(
            lambda: (parts.at[where(2, by_left[number]), :], from_right.at[number]), left
        )

    def to_right(dzh, source):
        rights[dzh] = send.copy(lambda: (source(), full_left.at[dzh]), right)

    def to_left(dzh, source):
        lefts[dzh] = send.copy(lambda: (source(), full_right.at[dzh]), left)

    def plain():
        to_right(3, lambda: parts.at[where(1, 3), :])
        to_left(2, lambda: parts.at[where(-1, 2), :])

    def merge_right(number):
        dzh = by_right[number]
        firsts[dzh].wait_recv()
        merged[dzh] = (
            parts[where(1, dzh), :].astype(F32) + from_left[number].astype(F32)
        ).astype(BF16)
        to_right(dzh, lambda: merged.at[dzh])

    def merge_left(number):
        dzh = by_left[number]
        firsts[dzh].wait_recv()
        merged[dzh] = (
            parts[where(-1, dzh), :].astype(F32) + from_right[number].astype(F32)
        ).astype(BF16)
        to_left(dzh, lambda: merged.at[dzh])

    def merge():
        merge_right(0)
        merge_left(0)

    def late():
        to_left(1, lambda: parts.at[where(-1, 1), :])
        merge_right(1)

    def last():
        to_right(0, lambda: parts.at[where(1, 0), :])
        merge_left(1)

    def complete(dzh):
        rights[dzh].wait_recv()
        lefts[dzh].wait_recv()
        summed = (
            parts[where(0, dzh), :].astype(F32)
            + full_left[dzh].astype(F32)
            + full_right[dzh].astype(F32)
        )
        if dzh:
            slot = level_of[dzh]
            level_send[slot] = summed.astype(BF16)
            levels[slot] = send.copy(
                lambda: (level_send.at[slot], level_recv.at[slot]), around.levels[slot]
            )
        else:
            total[...] = summed

    def end():
        for slot in range(3):
            levels[slot].wait_recv()
        result[...] = (
            total[...]
            + level_recv[0].astype(F32)
            + level_recv[1].astype(F32)
            + level_recv[2].astype(F32)
        ).astype(BF16)

    steps = {"plain": plain, "merge": merge, "late": late, "last": last, "end": end}
    for number in range(2):
        steps[f"first{number}"] = functools.partial(first, number)
    for dzh in range(4):
        steps[f"sum{dzh}"] = functools.partial(complete, dzh)
    return steps


def spread_steps(around, send, gathered, by_right):
    here = around.here
    right, left = around.beside[0], around.beside[2]
    up, ring_right, ring_left, relays = {}, {}, {}, []
    came = {0: 2, 1: 3, 2: 1}

    def move(dy, dzh, device):
        def ends():
            block = gathered.at[pl.ds(here.at(dy=dy, dzh=dzh)[1] * 2, 2)]
            return block, block

        return send.copy(ends, device)

    def ring(dzh):
        ring_right[dzh] = move(0, dzh, right)
        ring_left[dzh] = move(0, dzh, left)

    def begin():
        up[1] = move(0, 0, around.levels[1])
        up[2] = move(0, 0, around.levels[2])
        ring(0)

    def pass_on(dzh, tile, device):
        def ends():
            block = gathered.at[here.at(dzh=dzh)[1] * 2 + tile]
            return block, block

        return send.copy(ends, device)

    def level(slot):
        if slot:
            up[slot].wait_recv()
            up[slot + 2] = pass_on(came[slot], slot - 1, around.levels[slot])
        else:
            up[3].wait_recv()
            up[4].wait_recv()
        ring(came[slot])
        if slot == 0:
            relays.append(move(0, 2, around.beside[1]))

    def relay(dzh):
        if dzh in by_right:
            ring_right[dzh].wait_recv()
            relays.append(move(-1, dzh, right))
        else:
            ring_left[dzh].wait_recv()
            relays.append(move(1, dzh, left))

    def end():
        for dzh in range(4):
            if dzh == 2 or dzh in by_right:
                ring_left[dzh].wait_recv()
            if dzh not in by_right:
                ring_right[dzh].wait_recv()
        for made in relays:
            made.wait_recv()

    steps = {"begin": begin, "end": end}
    for slot in range(3):
        steps[f"level{slot}"] = functools.partial(level, slot)
    for dzh in (0, 1, 3):
        steps[f"relay{dzh}"] = functools.partial(relay, dzh)
    return steps


def scatter_steps(around, send, parts, out, core_recv, sent, received):
    here = around.here
    cores, made = [], {}

    def begin():
        for step in range(2):
            start = here.scatter_groups[1][1 - step] * TILE
            cores.append(
                send.copy(
                    lambda start=start, step=step: (
                        parts.at[rows_at(start, 4 * OWNED), :], core_recv.at[step]
                    ),
                    around.other,
                )
            )

    def collect(dx, step):
        spot = here.scatter_spots[dx]
        mine = rows_at((here.scatter_groups[0][1 - step] + spot) * TILE, OWNED)
        theirs = rows_at(spot * TILE, OWNED)
        return parts[mine, :].astype(F32) + core_recv[step, theirs, :].astype(F32)

    def chips(step):
        cores[step].wait_recv()
        for dx in (2, 1, 3, 0):
            slot = 4 * step + dx
            if slot != 4:
                sent[slot] = collect(dx, step).astype(BF16)
                made[slot] = send.copy(
                    lambda slot=slot: (sent.at[slot], received.at[slot]),
                    here.at(dx=dx, dzl=1 - step),
                )

    def end():
        summed = collect(0, 1)
        for slot in made:
            made[slot].wait_recv()
        for slot in made:
            summed = summed + received[slot].astype(F32)
        out[...] = summed.astype(BF16)

    return {
        "cores": begin,
        "chips0": functools.partial(chips, 0),
        "chips1": functools.partial(chips, 1),
        "end": end,
    }


def weight_steps(
    around, send, term, grad_weight, term_core, term_across, term_x, term_y, term_z, chunk_sum
):
    here = around.here
    half_mine = here.core * 128
    half_other = 128 - half_mine
    quarter_mine = half_mine + here.zl * 64
    quarter_other = half_mine + 64 - here.zl * 64
    piece_mine = quarter_mine + here.x * 16
    state = {}

    def lines(start, size):
        return pl.ds(pl.multiple_of(start, size), size)

    def same(start, size, device):
        def ends():
            block = grad_weight.at[lines(start, size), :]
            return block, block

        return send.copy(ends, device)

    def core():
        state["core"] = send.copy(lambda: (term.at[lines(half_other, 128), :], term_core), around.other)

    def across():
        state["core"].wait_recv()
        mine = lines(half_mine, 128)
        term[mine, :] = term[mine, :] + term_core[...]
        state["across"] = send.copy(lambda: (term.at[lines(quarter_other, 64), :], term_across), around.across)

    def along():
        state["across"].wait_recv()
        mine = lines(quarter_mine, 64)
        term[mine, :] = term[mine, :] + term_across[...]
        state["x"] = [
            send.copy(lambda dx=dx: (term.at[lines(quarter_mine + lax.rem(here.x + dx, jnp.int32(4)) * 16, 16), :], term_x.at[dx - 1]), around.ahead[dx - 1])
            for dx in (1, 2, 3)
        ]

    def over_y():
        for made in state["x"]:
            made.wait_recv()
        chunk_sum[0] = term[lines(piece_mine, 16), :] + term_x[0] + term_x[1] + term_x[2]
        state["y"] = [
            send.copy(lambda slot=slot: (chunk_sum.at[0], term_y.at[slot]), around.beside[slot]) for slot in range(3)
        ]

    def over_z():
        for made in state["y"]:
            made.wait_recv()
        chunk_sum[1] = (chunk_sum[0] + term_y[1]) + (term_y[0] + term_y[2])
        state["z"] = [
            send.copy(lambda slot=slot: (chunk_sum.at[1], term_z.at[slot]), around.levels[slot]) for slot in range(3)
        ]

    def whole_x():
        for made in state["z"]:
            made.wait_recv()
        piece = lines(piece_mine, 16)
        grad_weight[piece, :] = (chunk_sum[1] + term_z[0]) + (term_z[1] + term_z[2])
        state["all_x"] = [same(piece_mine, 16, around.ahead[slot]) for slot in range(3)]

    def whole_across():
        for made in state["all_x"]:
            made.wait_recv()
        state["all_across"] = same(quarter_mine, 64, around.across)

    def whole_core():
        state["all_across"].wait_recv()
        state["all_core"] = same(half_mine, 128, around.other)

    def end():
        state["all_core"].wait_recv()

    found = (core, across, along, over_y, over_z, whole_x, whole_across, whole_core, end)
    return {f"weight{number}": step for number, step in enumerate(found)}


def run(streams, names):
    for name in names:
        stream, step = name.split(".")
        streams[stream][step]()


def layer_kernel(
    count, tile_row, tile_col, features, weight, cotangent, tiles,
    output, grad_weight, grad_input, *rest
):
    (
        sources, backs, parts, parts_back, held, prefix, running,
        reduce_scratch, scatter_scratch, results, grads,
        term, term_core, term_across, term_x, term_y, term_z, chunk_sum,
        plan_lines, plan, plan_sem, tile_sem, send_sems, recv_sems,
    ) = rest
    slots = held.shape[0]
    share = slots // LOADS
    loads = [
        pltpu.make_async_copy(
            tiles.at[pl.ds(number * share, share)],
            held.at[pl.ds(number * share, share)],
            tile_sem.at[number],
        )
        for number in range(LOADS)
    ]
    for load in loads:
        load.start()
    around = Around(Place())
    here = around.here
    barrier = pltpu.get_barrier_semaphore()
    devices = around.everyone()
    for device in devices:
        pl.semaphore_signal(barrier, inc=1, device_id=device, device_id_type=MESH)
    pl.semaphore_wait(barrier, len(devices))
    send = Sender(send_sems, recv_sems)
    columns = [pl.ds(half * HALF, HALF) for half in range(2)]

    def product(line, transposed, half, source, placed, services):
        contract = 0 if transposed else 1
        running[...] = jnp.zeros_like(running)

        def group(number, carry):
            for at, names in services:
                @pl.when(number == at)
                def _():
                    run(streams, names)

            for step in range(GROUP):
                slot = number * GROUP + step
                block = source[plan[line + 1, slot]]
                fresh = lax.dot_general(
                    held[plan[line, slot]],
                    block,
                    (((contract,), (0,)), ((), ())),
                    preferred_element_type=F32,
                )
                running[...] = fresh + plan[line + 2, slot].astype(F32) * running[...]
                prefix[slot] = running[...].astype(BF16)
            return carry

        lax.fori_loop(0, slots // GROUP, group, 0)

        def place(tile, carry):
            placed[rows_at(tile * TILE, TILE), :] = prefix[plan[line + 3, tile]]
            return carry

        lax.fori_loop(0, TILES, place, 0, unroll=4)

    streams = {}
    mine = here.gather_tiles[0][0]
    for half in range(2):
        for part in range(2):
            sources[half][mine + part] = features[pl.ds(part * TILE, TILE), columns[half]]
        streams[f"g{half}"] = gather_steps(around, send, sources[half])
        streams[f"r{half}"] = reduce_steps(
            around, send, parts[half], *[ref.at[half] for ref in reduce_scratch], results.at[half]
        )
        streams[f"s{half}"] = spread_steps(around, send, backs[half], BY_RIGHT[half])
        streams[f"c{half}"] = scatter_steps(
            around, send, parts_back[half], grads.at[half],
            *[ref.at[half] for ref in scatter_scratch],
        )
    streams["w"] = weight_steps(
        around, send, term, grad_weight, term_core, term_across, term_x, term_y, term_z, chunk_sum
    )
    run(streams, GATHER_BEGIN)
    prefix[slots] = jnp.zeros((TILE, HALF), BF16)
    live = count[0]
    rows = tile_row[...]
    cols = tile_col[...]
    found = arrange(rows, gather_place(cols), live) + arrange(scatter_place(cols), rows, live)
    for line, value in enumerate(found):
        plan_lines[line : line + 1, :] = value
    load_plan = pltpu.make_async_copy(plan_lines, plan, plan_sem)
    load_plan.start()
    run(streams, GATHER_FIRST)
    for load in loads:
        load.wait()
    load_plan.wait()
    product(0, False, 0, sources[0], parts[0], GATHER_DURING)
    run(streams, GATHER_LAST)
    run(streams, REDUCE_FIRST)
    product(0, False, 1, sources[1], parts[1], REDUCE_DURING)
    run(streams, REDUCE_LAST)

    gathered = jnp.concatenate([results[0], results[1]], axis=1)
    preact = jnp.dot(gathered, weight[...], preferred_element_type=F32)
    squared = preact * preact
    bent = jnp.tanh(SLOPE * (preact + 0.044715 * (preact * squared)))
    slope = 0.5 * (1.0 + bent) + 0.5 * preact * (1.0 - bent * bent) * (
        SLOPE * (1.0 + 3 * 0.044715 * squared)
    )
    delta = (cotangent[...].astype(F32) * slope).astype(BF16)
    back = lax.dot_general(
        delta, weight[...], (((1,), (1,)), ((), ())), preferred_element_type=F32
    ).astype(BF16)
    mine = here.at()[1] * 2
    for half in range(2):
        for part in range(2):
            backs[half][mine + part] = back[
                part * TILE : (part + 1) * TILE, half * HALF : (half + 1) * HALF
            ]
    run(streams, SPREAD_BEGIN)
    output[...] = (0.5 * preact * (1.0 + bent)).astype(BF16)
    term[...] = lax.dot_general(
        gathered, delta, (((0,), (0,)), ((), ())), preferred_element_type=F32
    )
    run(streams, SPREAD_FIRST)
    product(4, True, 0, backs[0], parts_back[0], SPREAD_DURING)
    run(streams, SPREAD_LAST)
    product(4, True, 1, backs[1], parts_back[1], SCATTER_DURING)
    run(streams, SCATTER_LAST)
    for half in range(2):
        grad_input[:, columns[half]] = grads[half]
    send.finish()


def layer(count, tile_row, tile_col, features, weight, cotangent, tiles):
    slots = tiles.shape[0]
    block = (TILE, HALF)
    full = (OWNED, HALF)
    nodes = pltpu.VMEM((NODES, HALF), BF16)
    stacked = pltpu.VMEM((TILES, TILE, HALF), BF16)

    single = pltpu.VMEM((2,) + full, BF16)

    def pair(lead):
        return pltpu.VMEM((2, lead) + full, BF16)

    return pl.pallas_call(
        layer_kernel,
        out_shape=(
            jax.ShapeDtypeStruct((OWNED, WIDTH), BF16),
            jax.ShapeDtypeStruct((WIDTH, WIDTH), F32),
            jax.ShapeDtypeStruct((OWNED, WIDTH), BF16),
        ),
        in_specs=[SMEM_SPEC] + [VMEM_SPEC] * 5 + [ANY_SPEC],
        out_specs=(VMEM_SPEC,) * 3,
        scratch_shapes=[
            [stacked, stacked],
            [stacked, stacked],
            [nodes, nodes],
            [nodes, nodes],
            pltpu.VMEM((slots, TILE, TILE), BF16),
            pltpu.VMEM((slots + 1,) + block, BF16),
            pltpu.VMEM(block, F32),
            [pair(lead) for lead in (2, 2, 4, 4, 4, 3, 3)] + [pltpu.VMEM((2,) + full, F32)],
            [pltpu.VMEM((2, 2, 4 * OWNED, HALF), BF16), pair(8), pair(8)],
            single,
            single,
            pltpu.VMEM((WIDTH, WIDTH), F32),
            pltpu.VMEM((128, WIDTH), F32),
            pltpu.VMEM((64, WIDTH), F32),
            pltpu.VMEM((3, 16, WIDTH), F32),
            pltpu.VMEM((3, 16, WIDTH), F32),
            pltpu.VMEM((3, 16, WIDTH), F32),
            pltpu.VMEM((2, 16, WIDTH), F32),
            pltpu.VMEM((8, slots), jnp.int32),
            pltpu.SMEM((8, slots), jnp.int32),
            pltpu.SemaphoreType.DMA,
            pltpu.SemaphoreType.DMA((LOADS,)),
            pltpu.SemaphoreType.DMA((COPIES,)),
            pltpu.SemaphoreType.DMA((COPIES,)),
        ],
        compiler_params=pltpu.CompilerParams(
            collective_id=0, has_side_effects=True, vmem_limit_bytes=VMEM_LIMIT
        ),
        name="layer",
    )(count, tile_row, tile_col, features, weight, cotangent, tiles)


def hand_on_kernel(*refs):
    for number in range(3):
        refs[number + 3][...] = refs[number][...]


def hand_on(*arrays):
    return pl.pallas_call(
        hand_on_kernel,
        out_shape=tuple(jax.ShapeDtypeStruct(array.shape, array.dtype) for array in arrays),
        in_specs=[VMEM_SPEC] * 3,
        out_specs=(VMEM_SPEC,) * 3,
        name="hand_on",
    )(*arrays)


def shards(features, weight, adjacency, tile_row, tile_col, tile_count, cotangent):
    return hand_on(
        *layer(
            tile_count[0], tile_row[0], tile_col[0], features, weight, cotangent, adjacency[0, 0]
        )
    )


def solution(mesh):
    return jax.shard_map(
        shards,
        mesh=mesh,
        in_specs=(
            P(("row", "col"), None),
            P(),
            P("row", "col", None, None, None),
            P("row", "col", None),
            P("row", "col", None),
            P("row", "col"),
            P(("row", "col"), None),
        ),
        out_specs=(P(("row", "col"), None), P(), P(("row", "col"), None)),
        check_vma=False,
    )
```
